256 devices in a mesh: dp: 8 (over z), shard: 32 (over x, y, core).
Axes of the slice: x: 4, y: 4, z: 8, core: 2. Of those that a mesh axis runs over, the one named last changes fastest.
Arguments:
- activations: bfloat16 [8192, 8192], P('dp', 'shard'), may hold values from -6 to 6
- cotangent: bfloat16 [8192, 2048], P('dp'), may hold values from -0.0625 to 0.0625
- master: float32 [2048, 8192], P('dp', 'shard'), may hold values from -0.18 to 0.18
- adamw_first_moment: float32 [2048, 8192], P('dp', 'shard'), may hold values from -4 to 4
- second_moment: float32 [2048, 8192], P('dp', 'shard'), may hold values from 0.01 to 1
- new_owner: int32 [8, 1024, 1], P('dp', 'shard'), may hold values from 0 to 27; in each aligned block of 32 rows (0 to 31, 32 to 63, ..., all dimensions but the last counted through in order) at most 2 rows name the same one
Outputs:
- weights: bfloat16 [2048, 8192], P('dp')
- moved_master: float32 [8, 32, 32, 2, 8, 256], P('dp', 'shard')
- moved_first: float32 [8, 32, 32, 2, 8, 256], P('dp', 'shard')
- moved_second: float32 [8, 32, 32, 2, 8, 256], P('dp', 'shard')
The draws below stay inside these ranges and needn't reach their ends.
Inputs may be any that keep to these rules, and one draw needn't show every extreme that they name: `new_owner`: among the 32 blocks of one data index and one shard index no owner appears more than 2 times, and some owner appears exactly 2 times. Shard indices 28 and above own nothing.
All inputs are finite; a program needn't handle non-finite values.
Results may differ from the reference program's by a relative error of at most 0.007.
Values may be sent and summed in bfloat16 or wider, within the bound.
A program may use at most 64 MiB of HBM per device.

```python
import math
import jax
import jax.numpy as jnp
import numpy as np
from jax import lax

D = 8192
KV = 2048
NB = 32
TOKENS = 8192
DC = 256
G = 8
SURV = 28
MOST = 2
N_DP = 8
N_SHARD = 32


def block_scale(own_key, dims, pieces, smallest, top_value):
    factor_of, own = 1.0, jax.random.fold_in(own_key, 6)
    for dim, shards_of in pieces:
        heights = jnp.exp(jax.random.uniform(jax.random.fold_in(own, dim), (shards_of,), jnp.float32, smallest / len(pieces), top_value / len(pieces)))
        factor_of = factor_of * jnp.repeat(heights, dims[dim] // shards_of).reshape([-1 if axis == dim else 1 for axis in range(len(dims))])
    return factor_of


def shared_out(key, own, number, rows, count, top, limit, slope):
    ranking = jax.random.permutation(key, count)
    crowded, common = load_shares(count, rows * top, limit, slope, True), load_shares(count, rows * top, limit, slope, False)
    places = jnp.arange(count)

    def named(lengths, offset_by):
        used = int((lengths > 0).sum())
        fixed = max(1, used // 4)
        shifted = fixed + (places - fixed + offset_by * (used - fixed)) % max(1, count - fixed)
        return jnp.zeros((count,), jnp.int32).at[ranking[jnp.where(places < fixed, places, shifted)]].set(jnp.asarray(lengths, jnp.int32))

    lengths = jnp.where(number % 4 == 0, named(crowded, number // 4), named(common, number - number // 4 - 1))
    mixed = jax.random.permutation(jax.random.fold_in(own, 3), count)
    source_of, sink = mixed[0:count // 2 * 2:2], mixed[1:count // 2 * 2:2]
    slack = jnp.minimum(lengths[source_of] - 1, limit - lengths[sink]) // 2
    slack = jnp.where((source_of == ranking[0]) | (sink == ranking[0]) | (lengths[sink] == 0), 0, jnp.maximum(slack, 0))
    shifted = jax.random.randint(jax.random.fold_in(own, 4), (count // 2,), 0, 1 << 20) % (slack + 1)
    lengths = lengths.at[source_of].add(-shifted).at[sink].add(shifted)
    items = jnp.searchsorted(jnp.cumsum(lengths), jnp.arange(rows * top), side="right").astype(jnp.int32)
    listing = items.reshape(top, rows).T
    listing = listing[jax.random.permutation(jax.random.fold_in(own, 1), rows)]
    offset_by = jax.random.randint(jax.random.fold_in(own, 2), (rows, 1), 0, top)
    return jnp.take_along_axis(listing, (jnp.arange(top)[None, :] + offset_by) % top, axis=1)


def load_shares(count, total, bound, slope, full):
    weights = [(1 << 20) // math.isqrt(rank ** slope) + 1 for rank in range(1, count + 1)]
    largest = bound if full else min(bound, max(-(-total // count), total * weights[0] // sum(weights)))
    least = 1 if total - largest >= count - 1 else 0
    counts, surplus = [largest] + [least] * (count - 1), total - largest - least * (count - 1)
    while surplus > 0:
        candidates = [i for i in range(1, count) if counts[i] < largest] or [i for i in range(1, count) if counts[i] < bound]
        whole, left = sum([weights[i] for i in candidates]), surplus
        for i in candidates:
            addition = min(bound - counts[i], max(1, left * weights[i] // whole), surplus)
            counts[i] = counts[i] + addition
            surplus = surplus - addition
    return np.array(counts)


def bell_draw(rng, dims, deviation, most, cuts=(), held_as=jnp.bfloat16):
    result = deviation * jax.random.normal(rng, dims, jnp.float32)
    if cuts:
        result = result * block_scale(rng, dims, cuts, -0.22, 0.18)
    return jnp.clip(result, -most, most).astype(held_as)


def setup_inputs(seed: int = 0) -> dict:
    keys = jax.random.split(jax.random.key(seed), 7)
    activations = bell_draw(keys[0], (TOKENS, D), 1.0, 6.0, ((0, 8), (1, 32)))
    cotangent = bell_draw(keys[1], (TOKENS, KV), TOKENS ** -0.5, 0.0625, ((0, 8),))
    master = bell_draw(keys[2], (KV, D), 0.03, 0.18, ((0, 8), (1, 32)), jnp.float32)
    adamw_first_moment = bell_draw(keys[3], (KV, D), 0.5, 4.0, ((0, 8), (1, 32)), jnp.float32)
    second_moment = jnp.clip(jnp.exp(math.log(1.0) - 4.6051702 * jax.random.uniform(keys[4], (KV, D), jnp.float32) ** block_scale(keys[4], (KV, D), ((0, 8), (1, 32)), -0.2, 0.2)), 0.01, 1.0)
    new_owner_keys = jax.random.split(jax.random.fold_in(keys[5], 1), N_DP * (N_SHARD * NB) // NB)
    new_owner_turns = jax.random.permutation(jax.random.fold_in(keys[5], 3), N_DP * (N_SHARD * NB) // NB)
    new_owner = jax.vmap(lambda own, number: shared_out(jax.random.fold_in(keys[5], 2), own, number, NB, SURV, 1, MOST, 2))(new_owner_keys, new_owner_turns).reshape((N_DP, N_SHARD * NB, 1))
    return {"activations": activations, "cotangent": cotangent, "master": master, "adamw_first_moment": adamw_first_moment, "second_moment": second_moment, "new_owner": new_owner}


beta_one = 0.9
beta_two = 0.95
learning_rate = 0.003
decay_rate = 0.1
epsilon_value = 1e-08
adam_step = 100

def adam_update(master, adamw_first_moment, second_moment, gradient):
    corr_one = 1.0 - beta_one ** adam_step
    corr_two = 1.0 - beta_two ** adam_step
    first_new = beta_one * adamw_first_moment + (1.0 - beta_one) * gradient
    second_new = beta_two * second_moment + (1.0 - beta_two) * gradient * gradient
    direction = first_new / corr_one / (jnp.sqrt(second_new / corr_two) + epsilon_value)
    updated_master_weight = master - learning_rate * (direction + decay_rate * master)
    return (updated_master_weight, first_new, second_new)

def relocate(values_in, new_owner):
    blocks = values_in.reshape(N_DP, NB, G, N_SHARD, DC).transpose(0, 3, 1, 2, 4)
    owner_ids = new_owner[:, :, 0].reshape(N_DP, N_SHARD, NB).astype(jnp.int32)
    same_owner = owner_ids[:, :, :, None] == owner_ids[:, :, None, :]
    earlier = jnp.arange(NB)[None, :] < jnp.arange(NB)[:, None]
    slot_rank = lax.optimization_barrier(jnp.sum(jnp.where(same_owner & earlier[None, None], 1, 0), axis=3)).astype(jnp.int32)
    data_index = jnp.broadcast_to(jnp.arange(N_DP, dtype=jnp.int32)[:, None, None], owner_ids.shape)
    source_index = jnp.broadcast_to(jnp.arange(N_SHARD, dtype=jnp.int32)[None, :, None], owner_ids.shape)
    placed = jnp.zeros((N_DP, N_SHARD, N_SHARD, MOST, G, DC), jnp.float32)
    return placed.at[data_index, owner_ids, source_index, slot_rank].set(blocks)

def reference(activations, cotangent, master, adamw_first_moment, second_moment, new_owner):
    gradient = jnp.dot(cotangent.T, activations, preferred_element_type=jnp.float32)
    updated_master_weight, first_new, second_new = adam_update(master, adamw_first_moment, second_moment, gradient)
    weights = updated_master_weight.astype(jnp.bfloat16)
    return (weights, relocate(updated_master_weight, new_owner), relocate(first_new, new_owner), relocate(second_new, new_owner))
```

```python
import functools

import jax
import jax.numpy as jnp
from jax import lax
from jax.experimental import pallas as pl
from jax.experimental.pallas import tpu as pltpu
from jax.sharding import PartitionSpec as P

beta_one = 0.9
beta_two = 0.95
learning_rate = 0.003
decay_rate = 0.1
epsilon_value = 1e-08
adam_step = 100

MESH = pl.DeviceIdType.MESH
BF16 = jnp.bfloat16
F32 = jnp.float32

NZ = 8
NS = 32
OWNERS = 28
SLOT_ROWS = 16
C = 256
SUBS = 2
R = C // SUBS
H = R // 2


def adam_update(master, adamw_first_moment, second_moment, gradient):
    corr_one = 1.0 - beta_one**adam_step
    corr_two = 1.0 - beta_two**adam_step
    first_new = beta_one * adamw_first_moment + (1.0 - beta_one) * gradient
    second_new = beta_two * second_moment + (1.0 - beta_two) * gradient * gradient
    direction = first_new / corr_one / (jnp.sqrt(second_new / corr_two) + epsilon_value)
    updated_master_weight = master - learning_rate * (direction + decay_rate * master)
    return (updated_master_weight, first_new, second_new)


def exchange_kernel(
    act_hbm, cot_hbm, mas_hbm, fir_hbm, sec_hbm, own_ref,
    w_ref, out_mas, out_fir, out_sec,
    act, cot, mas, fir, sec, load_sem,
    pick, st_send, st_recv, g_send, g_recv,
    far_send, far_recv, mid_send, mid_recv, near_send, near_recv, two_send, two_recv,
    keep, grad,
    rs_send_sem, rs_recv_sem, ag_send_sem, ag_recv_sem, ag_half_sem, sib_sem,
    st_send_sem, st_recv_sem, g_send_sem, g_recv_sem,
):
    z = lax.axis_index("dp")
    me = lax.axis_index("shard")
    core = lax.rem(me, 2)
    y = lax.rem(lax.div(me, 2), 4)
    x = lax.div(me, 8)

    def at_z(step):
        return lax.rem(z + step + NZ, NZ)

    def plane(dx, dy, dc=0):
        return (lax.rem(x + dx + 4, 4) * 4 + lax.rem(y + dy + 4, 4)) * 2 + lax.rem(core + dc, 2)

    sibling = plane(0, 0, 1)

    order = (4, 3, 5, 1, 7, 2, 6, 0)
    loads = [pltpu.make_async_copy(act_hbm, act, load_sem.at[0])]
    cot_loads = {}
    for r in order:
        start = pl.multiple_of(at_z(r) * C, C)
        cot_loads[r] = pltpu.make_async_copy(
            cot_hbm.at[:, pl.ds(start, C)], cot.at[r], load_sem.at[1 + r]
        )
    state_loads = [
        pltpu.make_async_copy(mas_hbm, mas, load_sem.at[9]),
        pltpu.make_async_copy(fir_hbm, fir, load_sem.at[10]),
        pltpu.make_async_copy(sec_hbm, sec, load_sem.at[11]),
    ]
    loads[0].start()
    for r in order[:3]:
        cot_loads[r].start()
    for r in order[3:]:
        cot_loads[r].start()
    for load in state_loads:
        load.start()

    barrier = pltpu.get_barrier_semaphore()
    for step in (1, -1, 2, -2):
        pl.semaphore_signal(barrier, inc=1, device_id=(at_z(step), me), device_id_type=MESH)

    @pl.loop(1, NS)
    def _(i):
        pl.semaphore_signal(
            barrier, inc=1, device_id=(z, lax.rem(me + i, NS)), device_id_type=MESH
        )

    def partial(r):
        cot_loads[r].wait()
        return lax.dot_general(
            cot[r], act[...], (((0,), (0,)), ((), ())), preferred_element_type=F32
        )

    loads[0].wait()
    part = partial(4)
    far_send[...] = part.astype(BF16)
    mid_send[0] = partial(3).astype(BF16)
    mid_send[1] = partial(5).astype(BF16)

    pl.semaphore_wait(barrier, NS - 1 + 4)

    rs_sends = []

    def rs_copy(src, dst, index, step):
        copy = pltpu.make_async_remote_copy(
            src_ref=src, dst_ref=dst, send_sem=rs_send_sem.at[index], recv_sem=rs_recv_sem.at[index],
            device_id=(at_z(step), me), device_id_type=MESH,
        )
        return copy

    def far(sub, way):
        rows = pl.ds(sub * R + way * H, H)
        slot = pl.ds(sub * H, H)
        return rs_copy(far_send.at[rows], far_recv.at[way, slot], (sub * 4 + 0) * 2 + way, 2 - 4 * way)

    def mid(sub, way):
        rows = pl.ds(sub * R, R)
        return rs_copy(mid_send.at[way, rows], mid_recv.at[way, rows], (sub * 4 + 1) * 2 + way, 1 - 2 * way)

    def near(sub, way):
        rows = pl.ds(sub * R, R)
        return rs_copy(near_send.at[way, rows], near_recv.at[way, rows], (sub * 4 + 2) * 2 + way, 1 - 2 * way)

    def two(sub, way):
        rows = pl.ds(sub * R, R)
        return rs_copy(two_send.at[way, rows], two_recv.at[way, rows], (sub * 4 + 3) * 2 + way, 2 - 4 * way)

    def rs_start(copy):
        copy.start()
        rs_sends.append(copy)

    for sub in range(SUBS):
        for way in (0, 1):
            rs_start(far(sub, way))
            rs_start(mid(sub, way))

    keep[1] = partial(2)
    keep[2] = partial(6)
    near_send[0] = partial(1).astype(BF16)
    near_send[1] = partial(7).astype(BF16)
    for sub in range(SUBS):
        for way in (0, 1):
            rs_start(near(sub, way))
    keep[0] = partial(0)

    owner = own_ref[...].astype(F32)
    row_id = lax.broadcasted_iota(jnp.int32, (NS, NS), 0)
    col_id = lax.broadcasted_iota(jnp.int32, (NS, NS), 1)
    wide = jnp.broadcast_to(owner, (NS, NS))
    tall = jnp.sum(jnp.where(row_id == col_id, wide, 0.0), axis=1, keepdims=True)
    rank = jnp.sum(jnp.where((wide == tall) & (row_id < col_id), 1.0, 0.0), axis=0, keepdims=True)
    key = jnp.broadcast_to(owner * 2.0 + rank, (16, NS)).astype(BF16)
    spread = lax.broadcasted_iota(jnp.int32, (NS, C), 0) == lax.div(
        lax.broadcasted_iota(jnp.int32, (NS, C), 1), 8
    )
    slot_of = jnp.dot(key, spread.astype(F32).astype(BF16), preferred_element_type=F32)[0:1]
    within = lax.rem(lax.broadcasted_iota(jnp.int32, (1, C), 1), 8).astype(F32)
    target_row = slot_of * 8.0 + within
    slot_row = lax.broadcasted_iota(jnp.int32, (OWNERS * SLOT_ROWS, C), 0).astype(F32)
    pick[...] = jnp.where(slot_row == target_row, 1.0, 0.0).astype(BF16)

    for load in state_loads:
        load.wait()

    def packed(values):
        return (
            jnp.dot(pick[...], values, preferred_element_type=F32)
            .astype(BF16)
            .reshape(OWNERS, SLOT_ROWS, C)
        )

    st_send[:, 0] = packed(mas[...].astype(BF16))
    st_send[:, 1] = packed(fir[...].astype(BF16))
    st_send[:, 2] = packed(sec[...].astype(BF16))

    def st_copy(owner_id):
        return pltpu.make_async_remote_copy(
            src_ref=st_send.at[owner_id], dst_ref=st_recv.at[me],
            send_sem=st_send_sem.at[owner_id], recv_sem=st_recv_sem.at[me],
            device_id=(z, owner_id), device_id_type=MESH,
        )

    def g_copy(owner_id):
        return pltpu.make_async_remote_copy(
            src_ref=g_send.at[owner_id], dst_ref=g_recv.at[me],
            send_sem=g_send_sem.at[owner_id], recv_sem=g_recv_sem.at[me],
            device_id=(z, owner_id), device_id_type=MESH,
        )

    def to_owners(make, act_on):
        @pl.loop(1, NS)
        def _(i):
            owner_id = lax.rem(me + i, NS)

            @pl.when(owner_id < OWNERS)
            def _():
                act_on(make(owner_id))

    to_owners(st_copy, lambda copy: copy.start())

    for sub in range(SUBS):
        rows = pl.ds(sub * R, R)
        for way in (0, 1):
            far(sub, way).wait_recv()
            mid(sub, way).wait_recv()
            half = pl.ds(sub * R + way * H, H)
            keep[1 + way, rows] = keep[1 + way, rows] + mid_recv[way, rows].astype(F32)
            keep[1 + way, half] = keep[1 + way, half] + far_recv[way, pl.ds(sub * H, H)].astype(F32)
            two_send[way, rows] = keep[1 + way, rows].astype(BF16)
            rs_start(two(sub, way))

    ag_sends = []

    def ag_copy(sub, source, dx, dy, first=0, count=R, recv_sem=None):
        part_of = w_ref.at[source, pl.ds(sub * R + first, count)]
        copy = pltpu.make_async_remote_copy(
            src_ref=part_of, dst_ref=part_of,
            send_sem=ag_send_sem.at[len(ag_sends)],
            recv_sem=ag_recv_sem.at[sub, source] if recv_sem is None else recv_sem,
            device_id=(z, plane(dx, dy)), device_id_type=MESH,
        )
        copy.start()
        ag_sends.append(copy)

    def to_sibling(sub, source):
        part_of = w_ref.at[source, pl.ds(sub * R, R)]
        copy = pltpu.make_async_remote_copy(
            src_ref=part_of, dst_ref=part_of,
            send_sem=ag_send_sem.at[len(ag_sends)], recv_sem=sib_sem.at[sub, source],
            device_id=(z, sibling), device_id_type=MESH,
        )
        copy.start()
        ag_sends.append(copy)

    def arrived(sub, source, sem, first=0, count=R):
        part_of = w_ref.at[source, pl.ds(sub * R + first, count)]
        pltpu.make_async_remote_copy(
            src_ref=part_of, dst_ref=part_of, send_sem=sem, recv_sem=sem,
            device_id=(z, sibling), device_id_type=MESH,
        ).wait_recv()

    def update(sub):
        rows = pl.ds(sub * R, R)
        for way in (0, 1):
            near(sub, way).wait_recv()
            two(sub, way).wait_recv()
        total = keep[0, rows]
        for way in (0, 1):
            total = total + near_recv[way, rows].astype(F32) + two_recv[way, rows].astype(F32)
        new_master, _, _ = adam_update(mas[rows], fir[rows], sec[rows], total)
        w_ref[me, rows] = new_master.astype(BF16)
        grad[rows] = total.astype(BF16)
        for dx, dy in ((1, 0), (-1, 0), (0, 1), (0, -1), (2, 0), (0, 2)):
            ag_copy(sub, me, dx, dy)
        to_sibling(sub, me)

    def forward(sub):
        for (dx, dy), onward in (
            ((-1, 0), ((0, 1),)),
            ((1, 0), ((0, -1),)),
            ((0, -1), ((-1, 0),)),
            ((0, 1), ((1, 0),)),
        ):
            source = plane(dx, dy)
            arrived(sub, source, ag_recv_sem.at[sub, source])
            for to in onward:
                ag_copy(sub, source, *to)
            to_sibling(sub, source)
        source = plane(2, 0)
        arrived(sub, source, ag_recv_sem.at[sub, source])
        ag_copy(sub, source, 0, 2, 0, H, ag_half_sem.at[sub, 0])
        ag_copy(sub, source, 0, 1)
        ag_copy(sub, source, 0, -1)
        to_sibling(sub, source)
        source = plane(0, 2)
        arrived(sub, source, ag_recv_sem.at[sub, source])
        ag_copy(sub, source, 2, 0, H, H, ag_half_sem.at[sub, 1])
        ag_copy(sub, source, 1, 0)
        ag_copy(sub, source, -1, 0)
        to_sibling(sub, source)

    def finish(sub):
        for dx, dy in ((1, 1), (1, -1), (-1, 1), (-1, -1), (2, 1), (2, -1), (1, 2), (-1, 2)):
            source = plane(dx, dy)
            arrived(sub, source, ag_recv_sem.at[sub, source])
            to_sibling(sub, source)
        source = plane(2, 2)
        arrived(sub, source, ag_half_sem.at[sub, 0], 0, H)
        arrived(sub, source, ag_half_sem.at[sub, 1], H, H)
        to_sibling(sub, source)

    for sub in range(SUBS):
        update(sub)
        if sub < SUBS - 1:
            forward(sub)
        if sub >= 1:
            finish(sub - 1)

    g_send[...] = packed(grad[...])
    to_owners(g_copy, lambda copy: copy.start())
    forward(SUBS - 1)

    @pl.when(me < OWNERS)
    def _():
        st_recv[me] = st_send[me]
        g_recv[me] = g_send[me]

        @pl.loop(0, NS)
        def _(source):
            @pl.when(source != me)
            def _():
                for buffer, sem in ((st_recv, st_recv_sem), (g_recv, g_recv_sem)):
                    pltpu.make_async_remote_copy(
                        src_ref=buffer.at[source], dst_ref=buffer.at[source],
                        send_sem=sem.at[source], recv_sem=sem.at[source],
                        device_id=(z, sibling), device_id_type=MESH,
                    ).wait_recv()

            new_master, new_first, new_second = adam_update(
                st_recv[source, 0].astype(F32),
                st_recv[source, 1].astype(F32),
                st_recv[source, 2].astype(F32),
                g_recv[source].astype(F32),
            )
            out_mas[source] = new_master
            out_fir[source] = new_first
            out_sec[source] = new_second

    @pl.when(me >= OWNERS)
    def _():
        for out in (out_mas, out_fir, out_sec):
            out[...] = jnp.zeros_like(out)

    finish(SUBS - 1)

    for sub in range(SUBS):
        for dx in range(4):
            for dy in range(4):
                source = plane(dx, dy, 1)
                arrived(sub, source, sib_sem.at[sub, source])
    for copy in rs_sends + ag_sends:
        copy.wait_send()
    to_owners(st_copy, lambda copy: copy.wait_send())
    to_owners(g_copy, lambda copy: copy.wait_send())


def store_kernel(w_ref, mas_ref, fir_ref, sec_ref, weights, out_mas, out_fir, out_sec, sem):
    copies = [
        pltpu.make_async_copy(w_ref.at[s], weights.at[:, pl.ds(s * C, C)], sem.at[s])
        for s in range(NS)
    ]
    copies.append(pltpu.make_async_copy(mas_ref, out_mas, sem.at[NS]))
    copies.append(pltpu.make_async_copy(fir_ref, out_fir, sem.at[NS + 1]))
    copies.append(pltpu.make_async_copy(sec_ref, out_sec, sem.at[NS + 2]))
    for copy in copies:
        copy.start()
    for copy in copies:
        copy.wait()


def shards(activations, cotangent, master, adamw_first_moment, second_moment, new_owner):
    tokens = activations.shape[0]
    moved = (NS, SLOT_ROWS, C)
    hbm = pl.BlockSpec(memory_space=pl.ANY)
    vmem = pl.BlockSpec(memory_space=pltpu.VMEM)
    dma = pltpu.SemaphoreType.DMA
    gathered, mas, fir, sec = pl.pallas_call(
        exchange_kernel,
        out_shape=(
            pltpu.VMEM((NS, C, C), BF16),
            pltpu.VMEM(moved, F32),
            pltpu.VMEM(moved, F32),
            pltpu.VMEM(moved, F32),
        ),
        in_specs=[hbm] * 5 + [vmem],
        out_specs=[vmem] * 4,
        scratch_shapes=[
            pltpu.VMEM((tokens, C), BF16),
            pltpu.VMEM((NZ, tokens, C), BF16),
            pltpu.VMEM((C, C), F32),
            pltpu.VMEM((C, C), F32),
            pltpu.VMEM((C, C), F32),
            dma((12,)),
            pltpu.VMEM((OWNERS * SLOT_ROWS, C), BF16),
            pltpu.VMEM((OWNERS, 3, SLOT_ROWS, C), BF16),
            pltpu.VMEM((NS, 3, SLOT_ROWS, C), BF16),
            pltpu.VMEM((OWNERS, SLOT_ROWS, C), BF16),
            pltpu.VMEM((NS, SLOT_ROWS, C), BF16),
            pltpu.VMEM((C, C), BF16),
            pltpu.VMEM((2, C // 2, C), BF16),
            pltpu.VMEM((2, C, C), BF16),
            pltpu.VMEM((2, C, C), BF16),
            pltpu.VMEM((2, C, C), BF16),
            pltpu.VMEM((2, C, C), BF16),
            pltpu.VMEM((2, C, C), BF16),
            pltpu.VMEM((2, C, C), BF16),
            pltpu.VMEM((3, C, C), F32),
            pltpu.VMEM((C, C), BF16),
            dma((SUBS * 8,)),
            dma((SUBS * 8,)),
            dma((SUBS * 32,)),
            dma((SUBS, NS)),
            dma((SUBS, 2)),
            dma((SUBS, NS)),
            dma((NS,)),
            dma((NS,)),
            dma((NS,)),
            dma((NS,)),
        ],
        compiler_params=pltpu.CompilerParams(
            collective_id=0, has_side_effects=True, vmem_limit_bytes=40 * 2**20
        ),
        name="exchange",
    )(
        activations, cotangent, master, adamw_first_moment, second_moment,
        new_owner.reshape(1, NS),
    )
    weights, mas, fir, sec = pl.pallas_call(
        store_kernel,
        out_shape=(
            jax.ShapeDtypeStruct((C, NS * C), BF16),
            jax.ShapeDtypeStruct(moved, F32),
            jax.ShapeDtypeStruct(moved, F32),
            jax.ShapeDtypeStruct(moved, F32),
        ),
        in_specs=[vmem] * 4,
        out_specs=[hbm] * 4,
        scratch_shapes=[dma((NS + 3,))],
        name="store",
    )(gathered, mas, fir, sec)
    out_shape = (1, 1, NS, 2, SLOT_ROWS // 2, C)
    return (weights, mas.reshape(out_shape), fir.reshape(out_shape), sec.reshape(out_shape))


def solution(mesh):
    in_specs = (
        P("dp", "shard"),
        P("dp", None),
        P("dp", "shard"),
        P("dp", "shard"),
        P("dp", "shard"),
        P("dp", "shard", None),
    )
    out_specs = (
        P("dp", None),
        P("dp", "shard", None, None, None, None),
        P("dp", "shard", None, None, None, None),
        P("dp", "shard", None, None, None, None),
    )
    return jax.shard_map(shards, mesh=mesh, in_specs=in_specs, out_specs=out_specs, check_vma=False)
```

```python
import jax
import jax.numpy as jnp
from jax import lax
from jax.experimental import pallas as pl
from jax.experimental.pallas import tpu as pltpu
from jax.sharding import PartitionSpec as P

beta_one = 0.9
beta_two = 0.95
learning_rate = 0.003
decay_rate = 0.1
epsilon_value = 1e-08
adam_step = 100

MESH = pl.DeviceIdType.MESH
BF16 = jnp.bfloat16
F32 = jnp.float32

NZ = 8
NS = 32
CHIPS = 16
OWNERS = 28
SLOT_ROWS = 16
C = 256
SUBS = 4
R = C // SUBS
H = R // 2
CROSS = ((1, 0), (-1, 0), (0, 1), (0, -1), (2, 0), (0, 2))
ONWARD = (
    ((0, 1),),
    ((0, -1),),
    ((-1, 0),),
    ((1, 0),),
    ((0, 1), (0, -1)),
    ((1, 0), (-1, 0)),
)


def adam_update(master, adamw_first_moment, second_moment, gradient):
    corr_one = 1.0 - beta_one**adam_step
    corr_two = 1.0 - beta_two**adam_step
    first_new = beta_one * adamw_first_moment + (1.0 - beta_one) * gradient
    second_new = beta_two * second_moment + (1.0 - beta_two) * gradient * gradient
    direction = first_new / corr_one / (jnp.sqrt(second_new / corr_two) + epsilon_value)
    updated_master_weight = master - learning_rate * (direction + decay_rate * master)
    return (updated_master_weight, first_new, second_new)


def exchange_kernel(
    act_hbm, cot_hbm, mas_hbm, fir_hbm, sec_hbm, own_hbm,
    w_out, mas_out, fir_out, sec_out,
    act, cot, mas, fir, sec, own, load_sem,
    pick, st_send, st_land, st_cross, g_send, g_land, g_cross,
    far_send, far_recv, mid_send, mid_recv, near_send, near_recv, two_send, two_recv,
    keep, grad, own_w, new_mas, new_fir, new_sec,
    rs_send_sem, first_sem, last_sem, ag_send_sem, cross_sem, rest_sem, swap_send_sem, swap_sem,
    own_sem, move_send_sem, move_sem, move_swap_send_sem, move_swap_sem, out_sem,
):
    z = lax.axis_index("dp")
    me = lax.axis_index("shard")
    core = lax.rem(me, 2)
    chip = lax.div(me, 2)
    y = lax.rem(chip, 4)
    x = lax.div(chip, 4)

    def at_z(step):
        return lax.rem(z + step + NZ, NZ)

    def plane(dx, dy):
        return lax.rem(x + dx + 4, 4) * 4 + lax.rem(y + dy + 4, 4)

    def on_core(chip_id):
        return (z, chip_id * 2 + core)

    sibling = (z, chip * 2 + (1 - core))

    def remote(src, dst, send_sem, recv_sem, device):
        return pltpu.make_async_remote_copy(
            src_ref=src, dst_ref=dst, send_sem=send_sem, recv_sem=recv_sem,
            device_id=device, device_id_type=MESH,
        )

    def await_sent(ref, sem):
        remote(ref, ref, sem, sem, sibling).wait_send()

    def await_arrival(ref, sem):
        remote(ref, ref, sem, sem, sibling).wait_recv()

    def cot_load(r):
        start = pl.multiple_of(at_z(r) * C, C)
        return pltpu.make_async_copy(cot_hbm.at[:, pl.ds(start, C)], cot.at[r], load_sem.at[r])

    act_load = pltpu.make_async_copy(act_hbm, act, load_sem.at[8])
    state_loads = [
        pltpu.make_async_copy(own_hbm, own, load_sem.at[9]),
        pltpu.make_async_copy(mas_hbm, mas, load_sem.at[10]),
        pltpu.make_async_copy(fir_hbm, fir, load_sem.at[11]),
        pltpu.make_async_copy(sec_hbm, sec, load_sem.at[12]),
    ]
    act_load.start()
    for r in (4, 3, 5):
        cot_load(r).start()

    barrier = pltpu.get_barrier_semaphore()
    for step in (1, -1, 2, -2):
        pl.semaphore_signal(barrier, inc=1, device_id=(at_z(step), me), device_id_type=MESH)
    pl.semaphore_signal(barrier, inc=1, device_id=sibling, device_id_type=MESH)

    @pl.loop(1, CHIPS)
    def _(i):
        pl.semaphore_signal(
            barrier, inc=1, device_id=on_core(lax.rem(chip + i, CHIPS)), device_id_type=MESH
        )

    def partial(r):
        return lax.dot_general(
            cot[r], act[...], (((0,), (0,)), ((), ())), preferred_element_type=F32
        )

    act_load.wait()
    cot_load(4).wait()
    far_send[...] = partial(4).astype(BF16)
    cot_load(3).wait()
    cot_load(5).wait()
    for load in state_loads:
        load.start()
    for r in (2, 6, 1, 7, 0):
        cot_load(r).start()
    mid_send[0] = partial(3).astype(BF16)
    mid_send[1] = partial(5).astype(BF16)

    pl.semaphore_wait(barrier, 5 + CHIPS - 1)

    def rows_of(sub):
        return pl.ds(sub * R, R)

    def far_rows(sub, way):
        return pl.ds(sub * R + way * H, H)

    for sub in range(SUBS):
        for way in (0, 1):
            remote(
                far_send.at[far_rows(sub, way)], far_recv.at[way, pl.ds(sub * H, H)],
                rs_send_sem.at[0], first_sem.at[sub], (at_z(2 - 4 * way), me),
            ).start()
            remote(
                mid_send.at[way, rows_of(sub)], mid_recv.at[way, rows_of(sub)],
                rs_send_sem.at[0], first_sem.at[sub], (at_z(1 - 2 * way), me),
            ).start()

    for load in state_loads:
        load.wait()
    owner = own[...].astype(F32)
    row_id = lax.broadcasted_iota(jnp.int32, (NS, NS), 0)
    col_id = lax.broadcasted_iota(jnp.int32, (NS, NS), 1)
    wide = jnp.broadcast_to(owner, (NS, NS))
    tall = jnp.sum(jnp.where(row_id == col_id, wide, 0.0), axis=1, keepdims=True)
    rank = jnp.sum(jnp.where((wide == tall) & (row_id < col_id), 1.0, 0.0), axis=0, keepdims=True)
    key = jnp.broadcast_to(owner * 2.0 + rank, (16, NS)).astype(BF16)
    spread = lax.broadcasted_iota(jnp.int32, (NS, C), 0) == lax.div(
        lax.broadcasted_iota(jnp.int32, (NS, C), 1), 8
    )
    slot_of = jnp.dot(key, spread.astype(F32).astype(BF16), preferred_element_type=F32)[0:1]
    within = lax.rem(lax.broadcasted_iota(jnp.int32, (1, C), 1), 8).astype(F32)
    target_row = slot_of * 8.0 + within
    slot_row = lax.broadcasted_iota(jnp.int32, (OWNERS * SLOT_ROWS, C), 0).astype(F32)
    pick[...] = jnp.where(slot_row == target_row, 1.0, 0.0).astype(BF16)

    def packed(values):
        return (
            jnp.dot(pick[...], values, preferred_element_type=F32)
            .astype(BF16)
            .reshape(OWNERS // 2, 2, SLOT_ROWS, C)
        )

    st_send[:, :, 0] = packed(mas[...].astype(BF16))
    st_send[:, :, 1] = packed(fir[...].astype(BF16))
    st_send[:, :, 2] = packed(sec[...].astype(BF16))

    def move_out(send, land, index):
        @pl.loop(1, CHIPS)
        def _(i):
            to = lax.rem(chip + i, CHIPS)

            @pl.when(to < OWNERS // 2)
            def _():
                remote(
                    send.at[to], land.at[chip], move_send_sem.at[index], move_sem.at[index],
                    on_core(to),
                ).start()

        @pl.when(chip < OWNERS // 2)
        def _():
            land[chip] = send[chip]

    def move_across(land, cross, index):
        @pl.when(chip < OWNERS // 2)
        def _():
            await_arrival(land.at[pl.ds(0, CHIPS - 1)], move_sem.at[index])
            remote(
                land.at[:, 1 - core], cross, move_swap_send_sem.at[index], move_swap_sem.at[index],
                sibling,
            ).start()

    def move_sent(send, index):
        @pl.when(chip < OWNERS // 2)
        def _():
            await_sent(send.at[pl.ds(0, OWNERS // 2 - 1)], move_send_sem.at[index])

        @pl.when(chip >= OWNERS // 2)
        def _():
            await_sent(send, move_send_sem.at[index])

    move_out(st_send, st_land, 0)

    for r in (2, 6):
        cot_load(r).wait()
    keep[1] = partial(2)
    keep[2] = partial(6)
    for r in (1, 7):
        cot_load(r).wait()
    near_send[0] = partial(1).astype(BF16)
    near_send[1] = partial(7).astype(BF16)

    for sub in range(SUBS):
        await_arrival(w_out.at[pl.ds(0, 3), 0, rows_of(sub)], first_sem.at[sub])
        for way in (0, 1):
            both = pl.ds(sub * R + way * H, H)
            single = pl.ds(sub * R + (1 - way) * H, H)
            two_send[way, both] = (
                keep[1 + way, both]
                + mid_recv[way, both].astype(F32)
                + far_recv[way, pl.ds(sub * H, H)].astype(F32)
            ).astype(BF16)
            two_send[way, single] = (
                keep[1 + way, single] + mid_recv[way, single].astype(F32)
            ).astype(BF16)
            remote(
                two_send.at[way, rows_of(sub)], two_recv.at[way, rows_of(sub)],
                rs_send_sem.at[0], last_sem.at[sub], (at_z(2 - 4 * way), me),
            ).start()
        for way in (0, 1):
            remote(
                near_send.at[way, rows_of(sub)], near_recv.at[way, rows_of(sub)],
                rs_send_sem.at[0], last_sem.at[sub], (at_z(1 - 2 * way), me),
            ).start()

    cot_load(0).wait()
    keep[0] = partial(0)

    def gather_send(sub, src, source, to, sem, first=0, count=R):
        dst = w_out.at[source, core, pl.ds(sub * R + first, count)]
        remote(dst if src is None else src, dst, ag_send_sem.at[sub], sem, on_core(to)).start()

    def update(sub):
        rows = rows_of(sub)
        await_arrival(w_out.at[pl.ds(0, 4), 0, rows], last_sem.at[sub])
        total = keep[0, rows]
        for way in (0, 1):
            total = total + near_recv[way, rows].astype(F32) + two_recv[way, rows].astype(F32)
        new_master, _, _ = adam_update(mas[rows], fir[rows], sec[rows], total)
        own_w[rows] = new_master.astype(BF16)
        for index, (dx, dy) in enumerate(CROSS):
            gather_send(sub, own_w.at[rows], chip, plane(dx, dy), cross_sem.at[sub, index])
        pltpu.make_async_copy(own_w.at[rows], w_out.at[chip, core, rows], own_sem.at[sub]).start()
        grad[rows] = total.astype(BF16)

    def forward(sub):
        for index, (dx, dy) in enumerate(CROSS):
            source = plane(-dx, -dy)
            await_arrival(w_out.at[source, core, rows_of(sub)], cross_sem.at[sub, index])
            for tx, ty in ONWARD[index]:
                gather_send(sub, None, source, plane(tx, ty), rest_sem.at[sub])
        gather_send(sub, None, plane(2, 0), plane(0, 2), rest_sem.at[sub], 0, H)
        gather_send(sub, None, plane(0, 2), plane(2, 0), rest_sem.at[sub], H, H)

    def swap(sub):
        rows = rows_of(sub)
        await_arrival(w_out.at[pl.ds(0, 9), 0, rows], rest_sem.at[sub])
        pltpu.make_async_copy(own_w.at[rows], w_out.at[chip, core, rows], own_sem.at[sub]).wait()
        half = w_out.at[:, core, rows]
        remote(half, half, swap_send_sem.at[sub], swap_sem.at[sub], sibling).start()

    def settle(sub):
        await_arrival(w_out.at[:, 1 - core, rows_of(sub)], swap_sem.at[sub])
        await_sent(w_out.at[:, core, rows_of(sub)], swap_send_sem.at[sub])
        await_sent(w_out.at[pl.ds(0, 15), 0, rows_of(sub)], ag_send_sem.at[sub])

    def send_gradient():
        g_send[...] = packed(grad[...])
        move_out(g_send, g_land, 1)

    def own_blocks():
        @pl.when(chip < OWNERS // 2)
        def _():
            for cross, index in ((st_cross, 0), (g_cross, 1)):
                await_arrival(cross, move_swap_sem.at[index])

            @pl.loop(0, CHIPS)
            def _(source):
                for state, gradient, slot in (
                    (st_land.at[source, core], g_land.at[source, core], source * 2 + core),
                    (st_cross.at[source], g_cross.at[source], source * 2 + (1 - core)),
                ):
                    updated = adam_update(
                        state[0].astype(F32), state[1].astype(F32), state[2].astype(F32),
                        gradient[...].astype(F32),
                    )
                    new_mas[slot], new_fir[slot], new_sec[slot] = updated

        @pl.when(chip >= OWNERS // 2)
        def _():
            for new in (new_mas, new_fir, new_sec):
                new[...] = jnp.zeros_like(new)

        for index, (new, out) in enumerate(out_pairs):
            pltpu.make_async_copy(new, out, out_sem.at[index]).start()

    out_pairs = ((new_mas, mas_out), (new_fir, fir_out), (new_sec, sec_out))

    update(0)
    update(1)
    move_across(st_land, st_cross, 0)
    forward(0)
    update(2)
    forward(1)
    update(3)
    send_gradient()
    forward(2)
    swap(0)
    forward(3)
    swap(1)
    move_across(g_land, g_cross, 1)
    swap(2)
    own_blocks()
    swap(3)
    settle(0)
    settle(1)
    settle(2)
    settle(3)

    await_sent(w_out.at[pl.ds(0, 7), 0], rs_send_sem.at[0])
    for index, (new, out) in enumerate(out_pairs):
        pltpu.make_async_copy(new, out, out_sem.at[index]).wait()
    for index, (send, land, cross) in enumerate(
        ((st_send, st_land, st_cross), (g_send, g_land, g_cross))
    ):
        move_sent(send, index)

        @pl.when(chip < OWNERS // 2)
        def _():
            await_sent(cross, move_swap_send_sem.at[index])


def store_kernel(w_ref, mas_ref, fir_ref, sec_ref, weights, out_mas, out_fir, out_sec, sem):
    copies = [
        pltpu.make_async_copy(
            w_ref.at[s // 2, s % 2], weights.at[:, pl.ds(s * C, C)], sem.at[s]
        )
        for s in range(NS)
    ]
    copies.append(pltpu.make_async_copy(mas_ref, out_mas, sem.at[NS]))
    copies.append(pltpu.make_async_copy(fir_ref, out_fir, sem.at[NS + 1]))
    copies.append(pltpu.make_async_copy(sec_ref, out_sec, sem.at[NS + 2]))
    for copy in copies:
        copy.start()
    for copy in copies:
        copy.wait()


def shards(activations, cotangent, master, adamw_first_moment, second_moment, new_owner):
    tokens = activations.shape[0]
    moved = (NS, SLOT_ROWS, C)
    anywhere = pl.BlockSpec(memory_space=pl.ANY)
    vmem = pl.BlockSpec(memory_space=pltpu.VMEM)
    dma = pltpu.SemaphoreType.DMA
    gathered, mas, fir, sec = pl.pallas_call(
        exchange_kernel,
        out_shape=(
            pltpu.VMEM((CHIPS, 2, C, C), BF16),
            pltpu.VMEM(moved, F32),
            pltpu.VMEM(moved, F32),
            pltpu.VMEM(moved, F32),
        ),
        in_specs=[anywhere] * 6,
        out_specs=[anywhere] * 4,
        scratch_shapes=[
            pltpu.VMEM((tokens, C), BF16),
            pltpu.VMEM((NZ, tokens, C), BF16),
            pltpu.VMEM((C, C), F32),
            pltpu.VMEM((C, C), F32),
            pltpu.VMEM((C, C), F32),
            pltpu.VMEM((1, NS), jnp.int32),
            dma((13,)),
            pltpu.VMEM((OWNERS * SLOT_ROWS, C), BF16),
            pltpu.VMEM((OWNERS // 2, 2, 3, SLOT_ROWS, C), BF16),
            pltpu.VMEM((CHIPS, 2, 3, SLOT_ROWS, C), BF16),
            pltpu.VMEM((CHIPS, 3, SLOT_ROWS, C), BF16),
            pltpu.VMEM((OWNERS // 2, 2, SLOT_ROWS, C), BF16),
            pltpu.VMEM((CHIPS, 2, SLOT_ROWS, C), BF16),
            pltpu.VMEM((CHIPS, SLOT_ROWS, C), BF16),
            pltpu.VMEM((C, C), BF16),
            pltpu.VMEM((2, C // 2, C), BF16),
            pltpu.VMEM((2, C, C), BF16),
            pltpu.VMEM((2, C, C), BF16),
            pltpu.VMEM((2, C, C), BF16),
            pltpu.VMEM((2, C, C), BF16),
            pltpu.VMEM((2, C, C), BF16),
            pltpu.VMEM((2, C, C), BF16),
            pltpu.VMEM((3, C, C), F32),
            pltpu.VMEM((C, C), BF16),
            pltpu.VMEM((C, C), BF16),
            pltpu.VMEM(moved, F32),
            pltpu.VMEM(moved, F32),
            pltpu.VMEM(moved, F32),
            dma((1,)),
            dma((SUBS,)),
            dma((SUBS,)),
            dma((SUBS,)),
            dma((SUBS, len(CROSS))),
            dma((SUBS,)),
            dma((SUBS,)),
            dma((SUBS,)),
            dma((SUBS,)),
            dma((2,)),
            dma((2,)),
            dma((2,)),
            dma((2,)),
            dma((3,)),
        ],
        compiler_params=pltpu.CompilerParams(
            collective_id=0, has_side_effects=True, vmem_limit_bytes=40 * 2**20
        ),
        name="exchange",
    )(
        *[
            pltpu.with_memory_space_constraint(operand, pltpu.HBM)
            for operand in (
                activations, cotangent, master, adamw_first_moment, second_moment,
                new_owner.reshape(1, NS),
            )
        ]
    )
    weights, mas, fir, sec = pl.pallas_call(
        store_kernel,
        out_shape=(
            jax.ShapeDtypeStruct((C, NS * C), BF16),
            jax.ShapeDtypeStruct(moved, F32),
            jax.ShapeDtypeStruct(moved, F32),
            jax.ShapeDtypeStruct(moved, F32),
        ),
        in_specs=[vmem] * 4,
        out_specs=[anywhere] * 4,
        scratch_shapes=[dma((NS + 3,))],
        compiler_params=pltpu.CompilerParams(vmem_limit_bytes=8 * 2**20),
        name="store",
    )(
        *[
            pltpu.with_memory_space_constraint(operand, pltpu.VMEM)
            for operand in (gathered, mas, fir, sec)
        ]
    )
    out_shape = (1, 1, NS, 2, SLOT_ROWS // 2, C)
    return (weights, mas.reshape(out_shape), fir.reshape(out_shape), sec.reshape(out_shape))


def solution(mesh):
    in_specs = (
        P("dp", "shard"),
        P("dp", None),
        P("dp", "shard"),
        P("dp", "shard"),
        P("dp", "shard"),
        P("dp", "shard", None),
    )
    out_specs = (
        P("dp", None),
        P("dp", "shard", None, None, None, None),
        P("dp", "shard", None, None, None, None),
        P("dp", "shard", None, None, None, None),
    )
    return jax.shard_map(shards, mesh=mesh, in_specs=in_specs, out_specs=out_specs, check_vma=False)
```

```python
import jax
import jax.numpy as jnp
from jax import lax
from jax.experimental import pallas as pl
from jax.experimental.pallas import tpu as pltpu
from jax.sharding import PartitionSpec as P

beta_one = 0.9
beta_two = 0.95
learning_rate = 0.003
decay_rate = 0.1
epsilon_value = 1e-08
adam_step = 100

MESH = pl.DeviceIdType.MESH
BF16 = jnp.bfloat16
F32 = jnp.float32

NZ = 8
NS = 32
CHIPS = 16
OWNERS = 28
SLOT_ROWS = 16
C = 256
ROWS = (64, 64, 64, 64)
SUBS = len(ROWS)
START = tuple(sum(ROWS[:sub]) for sub in range(SUBS))
DIRECT = 4
CROSS = ((1, 0), (-1, 0), (0, 1), (0, -1), (2, 0), (0, 2))
ONWARD = (
    ((0, 1),),
    ((0, -1),),
    ((-1, 0),),
    ((1, 0),),
    ((0, 1), (0, -1)),
    ((1, 0), (-1, 0)),
)
FIRST_REST = (0, 1, 2, 3, 4, 6)


def moments(adamw_first_moment, second_moment, gradient):
    first_new = beta_one * adamw_first_moment + (1.0 - beta_one) * gradient
    second_new = beta_two * second_moment + (1.0 - beta_two) * gradient * gradient
    return first_new, second_new


def adam_update(master, adamw_first_moment, second_moment, gradient):
    corr_one = 1.0 - beta_one**adam_step
    corr_two = 1.0 - beta_two**adam_step
    first_new, second_new = moments(adamw_first_moment, second_moment, gradient)
    direction = first_new / corr_one / (jnp.sqrt(second_new / corr_two) + epsilon_value)
    return master - learning_rate * (direction + decay_rate * master)


def exchange_kernel(
    act_hbm, cot_hbm, mas_hbm, fir_hbm, sec_hbm, own_hbm,
    w_out, where_out, fir_out, sec_out,
    act, cot, mas, fir, sec, own, load_sem,
    own_line, own_land, own_cross, place, pick, st_send, st_land, st_cross, g_send, g_land, g_cross,
    far_send, far_recv, mid_send, mid_recv, near_send, near_recv, two_send, two_recv,
    keep, grad, own_w, new_fir, new_sec,
    rs_send_sem, first_sem, second_sem, last_sem, ag_send_sem, cross_sem, rest_sem, last_rest_sem, swap_send_sem, swap_sem,
    own_sem, move_send_sem, move_sem, move_swap_send_sem, move_swap_sem, out_sem,
):
    z = lax.axis_index("dp")
    me = lax.axis_index("shard")
    core = lax.rem(me, 2)
    chip = lax.div(me, 2)
    y = lax.rem(chip, 4)
    x = lax.div(chip, 4)

    def at_z(step):
        return lax.rem(z + step + NZ, NZ)

    def plane(dx, dy):
        return lax.rem(x + dx + 4, 4) * 4 + lax.rem(y + dy + 4, 4)

    def on_core(chip_id):
        return (z, chip_id * 2 + core)

    sibling = (z, chip * 2 + (1 - core))

    def remote(src, dst, send_sem, recv_sem, device):
        return pltpu.make_async_remote_copy(
            src_ref=src, dst_ref=dst, send_sem=send_sem, recv_sem=recv_sem,
            device_id=device, device_id_type=MESH,
        )

    def await_sent(ref, sem):
        remote(ref, ref, sem, sem, sibling).wait_send()

    def await_arrival(ref, sem):
        remote(ref, ref, sem, sem, sibling).wait_recv()

    def cot_load(r):
        start = pl.multiple_of(at_z(r) * C, C)
        return pltpu.make_async_copy(cot_hbm.at[:, pl.ds(start, C)], cot.at[r], load_sem.at[r])

    act_load = pltpu.make_async_copy(act_hbm, act, load_sem.at[8])
    state_loads = [
        pltpu.make_async_copy(own_hbm, own, load_sem.at[9]),
        pltpu.make_async_copy(mas_hbm, mas, load_sem.at[10]),
        pltpu.make_async_copy(fir_hbm, fir, load_sem.at[11]),
        pltpu.make_async_copy(sec_hbm, sec, load_sem.at[12]),
    ]
    act_load.start()
    for r in (4, 3, 5):
        cot_load(r).start()

    barrier = pltpu.get_barrier_semaphore()
    for step in (1, -1, 2, -2):
        pl.semaphore_signal(barrier, inc=1, device_id=(at_z(step), me), device_id_type=MESH)
    pl.semaphore_signal(barrier, inc=1, device_id=sibling, device_id_type=MESH)

    @pl.loop(1, CHIPS)
    def _(i):
        pl.semaphore_signal(
            barrier, inc=1, device_id=on_core(lax.rem(chip + i, CHIPS)), device_id_type=MESH
        )

    def partial(r):
        return lax.dot_general(
            cot[r], act[...], (((0,), (0,)), ((), ())), preferred_element_type=F32
        )

    act_load.wait()
    cot_load(4).wait()
    far_send[...] = partial(4).astype(BF16)
    cot_load(3).wait()
    cot_load(5).wait()
    for load in state_loads:
        load.start()
    for r in (2, 6, 1, 7, 0):
        cot_load(r).start()
    mid_send[0] = partial(3).astype(BF16)
    mid_send[1] = partial(5).astype(BF16)

    pl.semaphore_wait(barrier, 5 + CHIPS - 1)

    def rows_of(sub):
        return pl.ds(START[sub], ROWS[sub])

    def half_of(sub, way):
        return pl.ds(START[sub] + way * (ROWS[sub] // 2), ROWS[sub] // 2)

    def far_slot(sub):
        return pl.ds(START[sub] // 2, ROWS[sub] // 2)

    def reduce_first(sub):
        for way in (0, 1):
            remote(
                far_send.at[half_of(sub, way)], far_recv.at[way, far_slot(sub)],
                rs_send_sem.at[0], first_sem.at[sub], (at_z(2 - 4 * way), me),
            ).start()
            remote(
                mid_send.at[way, rows_of(sub)], mid_recv.at[way, rows_of(sub)],
                rs_send_sem.at[0], first_sem.at[sub], (at_z(1 - 2 * way), me),
            ).start()

    def multiply_two():
        for r in (2, 6):
            cot_load(r).wait()
        keep[1] = partial(2)
        keep[2] = partial(6)

    def multiply_one():
        for r in (1, 7):
            cot_load(r).wait()
        keep[3] = partial(1)
        keep[4] = partial(7)

    def multiply_own():
        cot_load(0).wait()
        keep[0] = partial(0)

    def send_near(sub, way):
        remote(
            near_send.at[way, rows_of(sub)], near_recv.at[way, rows_of(sub)],
            rs_send_sem.at[0], last_sem.at[sub], (at_z(1 - 2 * way), me),
        ).start()

    def reduce_second(sub):
        rows = rows_of(sub)
        direct = sub < DIRECT
        await_arrival(w_out.at[pl.ds(0, 3), 0, rows], first_sem.at[sub])
        for way in (0, 1):
            both = half_of(sub, way)
            single = half_of(sub, 1 - way)
            two_send[way, both] = (
                keep[1 + way, both]
                + mid_recv[way, both].astype(F32)
                + far_recv[way, far_slot(sub)].astype(F32)
            ).astype(BF16)
            two_send[way, single] = (
                keep[1 + way, single] + mid_recv[way, single].astype(F32)
            ).astype(BF16)
            remote(
                two_send.at[way, rows], two_recv.at[way, rows], rs_send_sem.at[0],
                last_sem.at[sub] if direct else second_sem.at[sub],
                (at_z((1 + direct) * (1 - 2 * way)), me),
            ).start()
        if direct:
            for way in (0, 1):
                near_send[way, rows] = keep[3 + way, rows].astype(BF16)
                send_near(sub, way)

    def reduce_third(sub):
        rows = rows_of(sub)
        await_arrival(w_out.at[pl.ds(0, 2), 0, rows], second_sem.at[sub])
        for way in (0, 1):
            near_send[way, rows] = (
                keep[3 + way, rows] + two_recv[way, rows].astype(F32)
            ).astype(BF16)
            send_near(sub, way)

    def packed(values):
        return (
            jnp.dot(pick[...], values, preferred_element_type=F32)
            .astype(BF16)
            .reshape(OWNERS // 2, 2, SLOT_ROWS, C)
        )

    def pack_state():
        for load in state_loads:
            load.wait()
        own_line[...] = jnp.full_like(own_line, -1)
        own_line[:, 0:NS] = own[...]
        move_out(own_line, own_land, 2, lambda to: own_line)
        owner = own[...].astype(F32)
        row_id = lax.broadcasted_iota(jnp.int32, (NS, NS), 0)
        col_id = lax.broadcasted_iota(jnp.int32, (NS, NS), 1)
        wide = jnp.broadcast_to(owner, (NS, NS))
        tall = jnp.sum(jnp.where(row_id == col_id, wide, 0.0), axis=1, keepdims=True)
        rank = jnp.sum(jnp.where((wide == tall) & (row_id < col_id), 1.0, 0.0), axis=0, keepdims=True)
        key = jnp.broadcast_to(owner * 2.0 + rank, (16, NS)).astype(BF16)
        spread = lax.broadcasted_iota(jnp.int32, (NS, C), 0) == lax.div(
            lax.broadcasted_iota(jnp.int32, (NS, C), 1), 8
        )
        slot_of = jnp.dot(key, spread.astype(F32).astype(BF16), preferred_element_type=F32)[0:1]
        within = lax.rem(lax.broadcasted_iota(jnp.int32, (1, C), 1), 8).astype(F32)
        target_row = slot_of * 8.0 + within
        slot_row = lax.broadcasted_iota(jnp.int32, (OWNERS * SLOT_ROWS, C), 0).astype(F32)
        pick[...] = jnp.where(slot_row == target_row, 1.0, 0.0).astype(BF16)

        st_send[:, :, 0] = packed(fir[...].astype(BF16))
        st_send[:, :, 1] = packed(sec[...].astype(BF16))
        move_out(st_send, st_land, 0)

    def move_out(send, land, index, piece=None):
        if piece is None:
            piece = lambda to: send.at[to]

        @pl.loop(1, CHIPS)
        def _(i):
            to = lax.rem(chip + i, CHIPS)

            @pl.when(to < OWNERS // 2)
            def _():
                remote(
                    piece(to), land.at[chip], move_send_sem.at[index], move_sem.at[index],
                    on_core(to),
                ).start()

        @pl.when(chip < OWNERS // 2)
        def _():
            land[chip] = piece(chip)[...]

    def move_across(land, cross, index):
        @pl.when(chip < OWNERS // 2)
        def _():
            await_arrival(land.at[pl.ds(0, CHIPS - 1)], move_sem.at[index])
            remote(
                land if index == 2 else land.at[:, 1 - core], cross,
                move_swap_send_sem.at[index], move_swap_sem.at[index], sibling,
            ).start()

    def move_sent(land, index):
        @pl.when(chip < OWNERS // 2)
        def _():
            await_sent(land.at[pl.ds(0, OWNERS // 2 - 1)], move_send_sem.at[index])

        @pl.when(chip >= OWNERS // 2)
        def _():
            await_sent(land.at[pl.ds(0, OWNERS // 2)], move_send_sem.at[index])

    def gather_send(sub, src, source, to, sem, rows=None):
        dst = w_out.at[source, core, rows_of(sub) if rows is None else rows]
        remote(dst if src is None else src, dst, ag_send_sem.at[sub], sem, on_core(to)).start()

    def update(sub):
        rows = rows_of(sub)
        direct = sub < DIRECT
        await_arrival(w_out.at[pl.ds(0, 2 + 2 * direct), 0, rows], last_sem.at[sub])
        total = keep[0, rows]
        for way in (0, 1):
            total = total + near_recv[way, rows].astype(F32)
            if direct:
                total = total + two_recv[way, rows].astype(F32)
        new_master = adam_update(mas[rows], fir[rows], sec[rows], total)
        own_w[rows] = new_master.astype(BF16)
        for index, (dx, dy) in enumerate(CROSS):
            gather_send(sub, own_w.at[rows], chip, plane(dx, dy), cross_sem.at[sub, index])
        pltpu.make_async_copy(own_w.at[rows], w_out.at[chip, core, rows], own_sem.at[sub]).start()
        if sub == SUBS - 1:
            swap_one(chip, own_w.at[rows])
        grad[rows] = total.astype(BF16)

    def forward(sub):
        for index, (dx, dy) in enumerate(CROSS):
            source = plane(-dx, -dy)
            await_arrival(w_out.at[source, core, rows_of(sub)], cross_sem.at[sub, index])
            for order, (tx, ty) in enumerate(ONWARD[index]):
                gather_send(
                    sub, None, source, plane(tx, ty), rest_arrival(sub, FIRST_REST[index] + order)
                )
            if index >= 4:
                gather_send(
                    sub, None, source, plane(dy, dx), rest_arrival(sub, 8), half_of(sub, index - 4)
                )
            if sub == SUBS - 1:
                swap_one(source)

    def rest_arrival(sub, order):
        return last_rest_sem.at[order] if sub == SUBS - 1 else rest_sem.at[sub]

    def swap_one(source, src=None):
        sub = SUBS - 1
        dst = w_out.at[source, core, rows_of(sub)]
        remote(
            dst if src is None else src, dst, swap_send_sem.at[sub], swap_sem.at[sub], sibling
        ).start()

    def swap(sub):
        rows = rows_of(sub)
        if sub < SUBS - 1:
            await_arrival(w_out.at[pl.ds(0, 9), 0, rows], rest_sem.at[sub])
            pltpu.make_async_copy(own_w.at[rows], w_out.at[chip, core, rows], own_sem.at[sub]).wait()
            half = w_out.at[:, core, rows]
            remote(half, half, swap_send_sem.at[sub], swap_sem.at[sub], sibling).start()
            return
        for index, (dx, dy) in enumerate(CROSS):
            for order, (tx, ty) in enumerate(ONWARD[index]):
                source = plane(-dx - tx, -dy - ty)
                await_arrival(
                    w_out.at[source, core, rows], rest_arrival(sub, FIRST_REST[index] + order)
                )
                swap_one(source)
        source = plane(2, 2)
        await_arrival(w_out.at[source, core, rows], rest_arrival(sub, 8))
        swap_one(source)
        pltpu.make_async_copy(own_w.at[rows], w_out.at[chip, core, rows], own_sem.at[sub]).wait()

    def settle(sub):
        await_arrival(w_out.at[:, 1 - core, rows_of(sub)], swap_sem.at[sub])
        await_sent(w_out.at[:, core, rows_of(sub)], swap_send_sem.at[sub])
        await_sent(w_out.at[pl.ds(0, 15), 0, rows_of(sub)], ag_send_sem.at[sub])

    def send_gradient():
        g_send[...] = packed(grad[...])
        move_out(g_send, g_land, 1)

    def find_places():
        place[...] = jnp.full_like(place, -1)

        @pl.when(chip < OWNERS // 2)
        def _():
            await_arrival(own_cross, move_swap_sem.at[2])
            lane = lax.broadcasted_iota(jnp.int32, (CHIPS, 128), 1)
            for index, owners in enumerate((own_land, own_cross)):
                mine = owners[...].reshape(CHIPS, 128) == me
                first = jnp.min(jnp.where(mine, lane, 128), axis=1, keepdims=True)
                last = jnp.max(jnp.where(mine, lane, -1), axis=1, keepdims=True)
                place[index] = jnp.where(
                    lane == 0,
                    jnp.where(first < 128, first, -1),
                    jnp.where((lane == 1) & (last > first), last, -1),
                )

        pltpu.make_async_copy(place, where_out, out_sem.at[2]).start()

    def own_blocks():
        @pl.when(chip < OWNERS // 2)
        def _():
            for cross, index in ((st_cross, 0), (g_cross, 1)):
                await_arrival(cross, move_swap_sem.at[index])

            @pl.loop(0, CHIPS)
            def _(source):
                for state, gradient, slot in (
                    (st_land.at[source, core], g_land.at[source, core], source * 2 + core),
                    (st_cross.at[source], g_cross.at[source], source * 2 + (1 - core)),
                ):
                    new_fir[slot], new_sec[slot] = moments(
                        state[0].astype(F32), state[1].astype(F32), gradient[...].astype(F32)
                    )

        @pl.when(chip >= OWNERS // 2)
        def _():
            for new in (new_fir, new_sec):
                new[...] = jnp.zeros_like(new)

        pltpu.make_async_copy(new_fir, fir_out, out_sem.at[0]).start()
        pltpu.make_async_copy(new_sec, sec_out, out_sem.at[1]).start()

    reduce_first(0)
    reduce_first(1)
    reduce_first(2)
    pack_state()
    multiply_two()
    multiply_one()
    reduce_second(0)
    reduce_first(3)
    multiply_own()
    reduce_second(1)
    reduce_second(2)
    update(0)
    reduce_second(3)
    update(1)
    forward(0)
    update(2)
    forward(1)
    update(3)
    pl.when(core == 0)(send_gradient)
    forward(2)
    move_across(own_land, own_cross, 2)
    move_across(st_land, st_cross, 0)
    swap(0)
    forward(3)
    pl.when(core == 1)(send_gradient)
    swap(1)
    move_across(g_land, g_cross, 1)
    swap(2)
    swap(3)
    find_places()
    own_blocks()
    settle(0)
    settle(1)
    settle(2)
    settle(3)

    await_sent(w_out.at[pl.ds(0, 7), 0], rs_send_sem.at[0])
    pltpu.make_async_copy(new_fir, fir_out, out_sem.at[0]).wait()
    pltpu.make_async_copy(new_sec, sec_out, out_sem.at[1]).wait()
    pltpu.make_async_copy(place, where_out, out_sem.at[2]).wait()
    for index, (land, cross) in enumerate(
        ((st_land, st_cross), (g_land, g_cross), (own_land, own_cross))
    ):
        move_sent(land, index)

        @pl.when(chip < OWNERS // 2)
        def _():
            await_sent(cross, move_swap_send_sem.at[index])


def store_kernel(
    w_ref, where_ref, fir_ref, sec_ref, weights, out_mas, out_fir, out_sec, new_mas, places, sem
):
    core = lax.rem(lax.axis_index("shard"), 2)
    where_copy = pltpu.make_async_copy(where_ref, places, sem.at[NS])
    where_copy.start()
    copies = [
        pltpu.make_async_copy(
            w_ref.at[s // 2, s % 2], weights.at[:, pl.ds(s * C, C)], sem.at[s]
        )
        for s in range(NS)
    ]
    copies.append(pltpu.make_async_copy(fir_ref, out_fir, sem.at[NS + 1]))
    copies.append(pltpu.make_async_copy(sec_ref, out_sec, sem.at[NS + 2]))
    for copy in copies:
        copy.start()

    where_copy.wait()

    @pl.loop(0, CHIPS)
    def _(source):
        for index in range(2):
            side = lax.rem(core + index, 2)
            for slot in range(2):
                block = places[index, source, slot]
                held = jnp.maximum(block, 0)
                start = pl.multiple_of(lax.div(held, 2) * 16, 16)
                tile = w_ref[source, side, pl.ds(start, 16)].astype(F32)
                rows = jnp.where(lax.rem(held, 2) == 1, tile[8:16], tile[0:8])
                new_mas[source * 2 + side, pl.ds(slot * 8, 8)] = jnp.where(block >= 0, rows, 0.0)

    copies.append(pltpu.make_async_copy(new_mas, out_mas, sem.at[NS + 3]))
    copies[-1].start()
    for copy in copies:
        copy.wait()


def shards(activations, cotangent, master, adamw_first_moment, second_moment, new_owner):
    tokens = activations.shape[0]
    moved = (NS, SLOT_ROWS, C)
    anywhere = pl.BlockSpec(memory_space=pl.ANY)
    vmem = pl.BlockSpec(memory_space=pltpu.VMEM)
    dma = pltpu.SemaphoreType.DMA
    gathered, where, fir, sec = pl.pallas_call(
        exchange_kernel,
        out_shape=(
            pltpu.VMEM((CHIPS, 2, C, C), BF16),
            pltpu.VMEM((2, CHIPS, 128), jnp.int32),
            pltpu.VMEM(moved, F32),
            pltpu.VMEM(moved, F32),
        ),
        in_specs=[anywhere] * 6,
        out_specs=[anywhere] * 4,
        scratch_shapes=[
            pltpu.VMEM((tokens, C), BF16),
            pltpu.VMEM((NZ, tokens, C), BF16),
            pltpu.VMEM((C, C), F32),
            pltpu.VMEM((C, C), F32),
            pltpu.VMEM((C, C), F32),
            pltpu.VMEM((1, NS), jnp.int32),
            dma((13,)),
            pltpu.VMEM((1, 128), jnp.int32),
            pltpu.VMEM((CHIPS, 1, 128), jnp.int32),
            pltpu.VMEM((CHIPS, 1, 128), jnp.int32),
            pltpu.VMEM((2, CHIPS, 128), jnp.int32),
            pltpu.VMEM((OWNERS * SLOT_ROWS, C), BF16),
            pltpu.VMEM((OWNERS // 2, 2, 2, SLOT_ROWS, C), BF16),
            pltpu.VMEM((CHIPS, 2, 2, SLOT_ROWS, C), BF16),
            pltpu.VMEM((CHIPS, 2, SLOT_ROWS, C), BF16),
            pltpu.VMEM((OWNERS // 2, 2, SLOT_ROWS, C), BF16),
            pltpu.VMEM((CHIPS, 2, SLOT_ROWS, C), BF16),
            pltpu.VMEM((CHIPS, SLOT_ROWS, C), BF16),
            pltpu.VMEM((C, C), BF16),
            pltpu.VMEM((2, C // 2, C), BF16),
            pltpu.VMEM((2, C, C), BF16),
            pltpu.VMEM((2, C, C), BF16),
            pltpu.VMEM((2, C, C), BF16),
            pltpu.VMEM((2, C, C), BF16),
            pltpu.VMEM((2, C, C), BF16),
            pltpu.VMEM((2, C, C), BF16),
            pltpu.VMEM((5, C, C), F32),
            pltpu.VMEM((C, C), BF16),
            pltpu.VMEM((C, C), BF16),
            pltpu.VMEM(moved, F32),
            pltpu.VMEM(moved, F32),
            dma((1,)),
            dma((SUBS,)),
            dma((SUBS,)),
            dma((SUBS,)),
            dma((SUBS,)),
            dma((SUBS, len(CROSS))),
            dma((SUBS,)),
            dma((9,)),
            dma((SUBS,)),
            dma((SUBS,)),
            dma((SUBS,)),
            dma((3,)),
            dma((3,)),
            dma((3,)),
            dma((3,)),
            dma((3,)),
        ],
        compiler_params=pltpu.CompilerParams(
            collective_id=0, has_side_effects=True, vmem_limit_bytes=40 * 2**20
        ),
        name="exchange",
    )(
        *[
            pltpu.with_memory_space_constraint(operand, pltpu.HBM)
            for operand in (
                activations, cotangent, master, adamw_first_moment, second_moment,
                new_owner.reshape(1, NS),
            )
        ]
    )
    weights, mas, fir, sec = pl.pallas_call(
        store_kernel,
        out_shape=(
            jax.ShapeDtypeStruct((C, NS * C), BF16),
            jax.ShapeDtypeStruct(moved, F32),
            jax.ShapeDtypeStruct(moved, F32),
            jax.ShapeDtypeStruct(moved, F32),
        ),
        in_specs=[vmem] * 4,
        out_specs=[anywhere] * 4,
        scratch_shapes=[
            pltpu.VMEM(moved, F32),
            pltpu.SMEM((2, CHIPS, 128), jnp.int32),
            dma((NS + 4,)),
        ],
        compiler_params=pltpu.CompilerParams(vmem_limit_bytes=8 * 2**20),
        name="store",
    )(
        *[
            pltpu.with_memory_space_constraint(operand, pltpu.VMEM)
            for operand in (gathered, where, fir, sec)
        ]
    )
    out_shape = (1, 1, NS, 2, SLOT_ROWS // 2, C)
    return (weights, mas.reshape(out_shape), fir.reshape(out_shape), sec.reshape(out_shape))


def solution(mesh):
    in_specs = (
        P("dp", "shard"),
        P("dp", None),
        P("dp", "shard"),
        P("dp", "shard"),
        P("dp", "shard"),
        P("dp", "shard", None),
    )
    out_specs = (
        P("dp", None),
        P("dp", "shard", None, None, None, None),
        P("dp", "shard", None, None, None, None),
        P("dp", "shard", None, None, None, None),
    )
    return jax.shard_map(shards, mesh=mesh, in_specs=in_specs, out_specs=out_specs, check_vma=False)
```

```python
import jax
import jax.numpy as jnp
from jax import lax
from jax.experimental import pallas as pl
from jax.experimental.pallas import tpu as pltpu
from jax.sharding import PartitionSpec as P

beta_one = 0.9
beta_two = 0.95
learning_rate = 0.003
decay_rate = 0.1
epsilon_value = 1e-08
adam_step = 100

MESH = pl.DeviceIdType.MESH
BF16 = jnp.bfloat16
F32 = jnp.float32

NZ = 8
ORDER = (4, 3, 5, 2, 6, 1, 7, 0)
NS = 32
CHIPS = 16
OWNERS = 28
SLOT_ROWS = 16
C = 256
ROWS = (64, 64, 64, 64)
SUBS = len(ROWS)
START = tuple(sum(ROWS[:sub]) for sub in range(SUBS))
CROSS = ((1, 0), (-1, 0), (0, 1), (0, -1), (2, 0), (0, 2))
ONWARD = (
    ((0, 1),),
    ((0, -1),),
    ((-1, 0),),
    ((1, 0),),
    ((0, 1), (0, -1)),
    ((1, 0), (-1, 0)),
)


def moments(adamw_first_moment, second_moment, gradient):
    first_new = beta_one * adamw_first_moment + (1.0 - beta_one) * gradient
    second_new = beta_two * second_moment + (1.0 - beta_two) * gradient * gradient
    return first_new, second_new


def adam_update(master, adamw_first_moment, second_moment, gradient):
    corr_one = 1.0 - beta_one**adam_step
    corr_two = 1.0 - beta_two**adam_step
    first_new, second_new = moments(adamw_first_moment, second_moment, gradient)
    direction = first_new / corr_one / (jnp.sqrt(second_new / corr_two) + epsilon_value)
    return master - learning_rate * (direction + decay_rate * master)


def exchange_kernel(
    act_hbm, cot_hbm, mas_hbm, fir_hbm, sec_hbm, own_hbm,
    w_out, where_out, fir_out, sec_out,
    act, cot, state, own, load_sem,
    own_line, own_land, own_cross, place, pick, st_send, st_land, st_cross, g_send, g_land, g_cross,
    far_send, far_recv, mid_send, mid_recv, near_send, near_recv, two_send, two_recv,
    keep, grad, own_w, new_fir, new_sec,
    rs_send_sem, first_sem, last_sem, ag_send_sem, cross_sem, rest_sem, swap_send_sem, swap_sem,
    own_sem, move_send_sem, move_sem, move_swap_send_sem, move_swap_sem, out_sem,
):
    z = lax.axis_index("dp")
    me = lax.axis_index("shard")
    core = lax.rem(me, 2)
    chip = lax.div(me, 2)
    y = lax.rem(chip, 4)
    x = lax.div(chip, 4)

    def at_z(step):
        return lax.rem(z + step + NZ, NZ)

    def plane(dx, dy):
        return lax.rem(x + dx + 4, 4) * 4 + lax.rem(y + dy + 4, 4)

    def on_core(chip_id):
        return (z, chip_id * 2 + core)

    sibling = (z, chip * 2 + (1 - core))

    def remote(src, dst, send_sem, recv_sem, device):
        return pltpu.make_async_remote_copy(
            src_ref=src, dst_ref=dst, send_sem=send_sem, recv_sem=recv_sem,
            device_id=device, device_id_type=MESH,
        )

    def await_sent(ref, sem):
        remote(ref, ref, sem, sem, sibling).wait_send()

    def await_arrival(ref, sem):
        remote(ref, ref, sem, sem, sibling).wait_recv()

    def cot_load(slot):
        start = pl.multiple_of(at_z(ORDER[slot]) * C, C)
        return pltpu.make_async_copy(
            cot_hbm.at[:, pl.ds(start, C)], cot.at[slot], load_sem.at[(slot + 1) // 2]
        )

    def await_cot(slot, count):
        ref = cot.at[pl.ds(slot, count)]
        pltpu.make_async_copy(ref, ref, load_sem.at[(slot + 1) // 2]).wait()

    act_load = pltpu.make_async_copy(act_hbm, act, load_sem.at[5])
    own_load = pltpu.make_async_copy(own_hbm, own, load_sem.at[6])
    mas, fir, sec = state.at[0], state.at[1], state.at[2]
    act_load.start()
    for slot in range(3):
        cot_load(slot).start()

    barrier = pltpu.get_barrier_semaphore()
    for step in (1, -1, 2, -2):
        pl.semaphore_signal(barrier, inc=1, device_id=(at_z(step), me), device_id_type=MESH)
    pl.semaphore_signal(barrier, inc=1, device_id=sibling, device_id_type=MESH)

    @pl.loop(1, CHIPS)
    def _(i):
        pl.semaphore_signal(
            barrier, inc=1, device_id=on_core(lax.rem(chip + i, CHIPS)), device_id_type=MESH
        )

    def partial(slot):
        return lax.dot_general(
            cot[slot], act[...], (((0,), (0,)), ((), ())), preferred_element_type=F32
        )

    act_load.wait()
    await_cot(0, 1)
    far_send[...] = partial(0).astype(BF16)
    await_cot(1, 2)
    own_load.start()
    for index, src in enumerate((mas_hbm, fir_hbm, sec_hbm)):
        pltpu.make_async_copy(src, state.at[index], load_sem.at[7]).start()
    for slot in range(3, NZ):
        cot_load(slot).start()
    mid_send[0] = partial(1).astype(BF16)
    mid_send[1] = partial(2).astype(BF16)

    pl.semaphore_wait(barrier, 5 + CHIPS - 1)

    def rows_of(sub):
        return pl.ds(START[sub], ROWS[sub])

    def half_of(sub, way):
        return pl.ds(START[sub] + way * (ROWS[sub] // 2), ROWS[sub] // 2)

    def far_slot(sub):
        return pl.ds(START[sub] // 2, ROWS[sub] // 2)

    def reduce_first(sub):
        for way in (0, 1):
            remote(
                far_send.at[half_of(sub, way)], far_recv.at[way, far_slot(sub)],
                rs_send_sem.at[0], first_sem.at[sub], (at_z(2 - 4 * way), me),
            ).start()
            remote(
                mid_send.at[way, rows_of(sub)], mid_recv.at[way, rows_of(sub)],
                rs_send_sem.at[0], first_sem.at[sub], (at_z(1 - 2 * way), me),
            ).start()

    def multiply_two():
        await_cot(3, 2)
        keep[1] = partial(3)
        keep[2] = partial(4)

    def multiply_one():
        await_cot(5, 2)
        near_send[0] = partial(5).astype(BF16)
        near_send[1] = partial(6).astype(BF16)

    def multiply_own():
        await_cot(7, 1)
        keep[0] = partial(7)

    def send_near(sub, way):
        remote(
            near_send.at[way, rows_of(sub)], near_recv.at[way, rows_of(sub)],
            rs_send_sem.at[0], last_sem.at[sub], (at_z(1 - 2 * way), me),
        ).start()

    def reduce_second(sub):
        rows = rows_of(sub)
        await_arrival(w_out.at[pl.ds(0, 3), 0, rows], first_sem.at[sub])
        for way in (0, 1):
            both = half_of(sub, way)
            single = half_of(sub, 1 - way)
            two_send[way, both] = (
                keep[1 + way, both]
                + mid_recv[way, both].astype(F32)
                + far_recv[way, far_slot(sub)].astype(F32)
            ).astype(BF16)
            two_send[way, single] = (
                keep[1 + way, single] + mid_recv[way, single].astype(F32)
            ).astype(BF16)
            remote(
                two_send.at[way, rows], two_recv.at[way, rows], rs_send_sem.at[0],
                last_sem.at[sub], (at_z(2 - 4 * way), me),
            ).start()
        for way in (0, 1):
            send_near(sub, way)

    def packed(values):
        return (
            jnp.dot(pick[...], values, preferred_element_type=F32)
            .astype(BF16)
            .reshape(OWNERS // 2, 2, SLOT_ROWS, C)
        )

    def pack_state():
        own_load.wait()
        pltpu.make_async_copy(state, state, load_sem.at[7]).wait()
        own_line[...] = jnp.full_like(own_line, -1)
        own_line[:, 0:NS] = own[...]
        move_out(own_line, own_land, 2, lambda to: own_line)
        owner = own[...].astype(F32)
        row_id = lax.broadcasted_iota(jnp.int32, (NS, NS), 0)
        col_id = lax.broadcasted_iota(jnp.int32, (NS, NS), 1)
        wide = jnp.broadcast_to(owner, (NS, NS))
        tall = jnp.sum(jnp.where(row_id == col_id, wide, 0.0), axis=1, keepdims=True)
        rank = jnp.sum(jnp.where((wide == tall) & (row_id < col_id), 1.0, 0.0), axis=0, keepdims=True)
        key = jnp.broadcast_to(owner * 2.0 + rank, (16, NS)).astype(BF16)
        spread = lax.broadcasted_iota(jnp.int32, (NS, C), 0) == lax.div(
            lax.broadcasted_iota(jnp.int32, (NS, C), 1), 8
        )
        slot_of = jnp.dot(key, spread.astype(F32).astype(BF16), preferred_element_type=F32)[0:1]
        within = lax.rem(lax.broadcasted_iota(jnp.int32, (1, C), 1), 8).astype(F32)
        target_row = slot_of * 8.0 + within
        slot_row = lax.broadcasted_iota(jnp.int32, (OWNERS * SLOT_ROWS, C), 0).astype(F32)
        pick[...] = jnp.where(slot_row == target_row, 1.0, 0.0).astype(BF16)

        st_send[:, :, 0] = packed(fir[...].astype(BF16))
        st_send[:, :, 1] = packed(sec[...].astype(BF16))
        move_out(st_send, st_land, 0)

    def move_out(send, land, index, piece=None):
        if piece is None:
            piece = lambda to: send.at[to]

        @pl.loop(1, CHIPS)
        def _(i):
            to = lax.rem(chip + i, CHIPS)

            @pl.when(to < OWNERS // 2)
            def _():
                remote(
                    piece(to), land.at[chip], move_send_sem.at[index], move_sem.at[index],
                    on_core(to),
                ).start()

        @pl.when(chip < OWNERS // 2)
        def _():
            land[chip] = piece(chip)[...]

    def move_across(land, cross, index):
        @pl.when(chip < OWNERS // 2)
        def _():
            await_arrival(land.at[pl.ds(0, CHIPS - 1)], move_sem.at[index])
            remote(
                land if index == 2 else land.at[:, 1 - core], cross,
                move_swap_send_sem.at[index], move_swap_sem.at[index], sibling,
            ).start()

    def move_sent(land, index):
        @pl.when(chip < OWNERS // 2)
        def _():
            await_sent(land.at[pl.ds(0, OWNERS // 2 - 1)], move_send_sem.at[index])

        @pl.when(chip >= OWNERS // 2)
        def _():
            await_sent(land.at[pl.ds(0, OWNERS // 2)], move_send_sem.at[index])

    def gather_send(sub, src, source, to, sem, rows=None):
        dst = w_out.at[source, core, rows_of(sub) if rows is None else rows]
        remote(dst if src is None else src, dst, ag_send_sem.at[0], sem, on_core(to)).start()

    def update(sub):
        rows = rows_of(sub)
        await_arrival(w_out.at[pl.ds(0, 4), 0, rows], last_sem.at[sub])
        total = keep[0, rows]
        for way in (0, 1):
            total = total + near_recv[way, rows].astype(F32) + two_recv[way, rows].astype(F32)
        new_master = adam_update(mas[rows], fir[rows], sec[rows], total)
        own_w[rows] = new_master.astype(BF16)
        for index, (dx, dy) in enumerate(CROSS):
            gather_send(sub, own_w.at[rows], chip, plane(dx, dy), cross_sem.at[sub, min(index, 4)])
        pltpu.make_async_copy(own_w.at[rows], w_out.at[chip, core, rows], own_sem.at[sub]).start()
        if sub == SUBS - 1:
            swap_one(chip, own_w.at[rows])
        grad[rows] = total.astype(BF16)

    def forward(sub):
        for index, (dx, dy) in enumerate(CROSS):
            source = plane(-dx, -dy)
            if index < 4:
                await_arrival(w_out.at[source, core, rows_of(sub)], cross_sem.at[sub, index])
            elif index == 4:
                await_arrival(w_out.at[pl.ds(0, 2), core, rows_of(sub)], cross_sem.at[sub, 4])
            for tx, ty in ONWARD[index]:
                gather_send(sub, None, source, plane(tx, ty), rest_arrival(sub, index // 4))
            if index >= 4:
                gather_send(
                    sub, None, source, plane(dy, dx), rest_arrival(sub, 2), half_of(sub, index - 4)
                )
            if sub == SUBS - 1:
                swap_one(source)

    def rest_arrival(sub, order):
        return rest_sem.at[sub + order if sub == SUBS - 1 else sub]

    def swap_one(source, src=None):
        sub = SUBS - 1
        dst = w_out.at[source, core, rows_of(sub)]
        remote(
            dst if src is None else src, dst, swap_send_sem.at[0], swap_sem.at[0], sibling
        ).start()

    def swap(sub):
        rows = rows_of(sub)
        if sub < SUBS - 1:
            await_arrival(w_out.at[pl.ds(0, 9), 0, rows], rest_sem.at[sub])
            pltpu.make_async_copy(own_w.at[rows], w_out.at[chip, core, rows], own_sem.at[sub]).wait()
            half = w_out.at[:, core, rows]
            remote(half, half, swap_send_sem.at[0], swap_sem.at[0], sibling).start()
            return
        for index, (dx, dy) in enumerate(CROSS):
            if index in (0, 4):
                await_arrival(w_out.at[pl.ds(0, 4), core, rows], rest_arrival(sub, index // 4))
            for tx, ty in ONWARD[index]:
                swap_one(plane(-dx - tx, -dy - ty))
        source = plane(2, 2)
        await_arrival(w_out.at[source, core, rows], rest_arrival(sub, 2))
        swap_one(source)
        pltpu.make_async_copy(own_w.at[rows], w_out.at[chip, core, rows], own_sem.at[sub]).wait()

    def settle():
        await_arrival(w_out.at[:, 1 - core], swap_sem.at[0])
        await_sent(w_out.at[:, core], swap_send_sem.at[0])
        await_sent(w_out.at[pl.ds(0, 15), core], ag_send_sem.at[0])

    def send_gradient():
        g_send[...] = packed(grad[...])
        move_out(g_send, g_land, 1)

    def find_places():
        place[...] = jnp.full_like(place, -1)

        @pl.when(chip < OWNERS // 2)
        def _():
            await_arrival(own_cross, move_swap_sem.at[2])
            lane = lax.broadcasted_iota(jnp.int32, (CHIPS, 128), 1)
            for index, owners in enumerate((own_land, own_cross)):
                mine = owners[...].reshape(CHIPS, 128) == me
                first = jnp.min(jnp.where(mine, lane, 128), axis=1, keepdims=True)
                last = jnp.max(jnp.where(mine, lane, -1), axis=1, keepdims=True)
                place[index] = jnp.where(
                    lane == 0,
                    jnp.where(first < 128, first, -1),
                    jnp.where((lane == 1) & (last > first), last, -1),
                )

        pltpu.make_async_copy(place, where_out, out_sem.at[2]).start()

    def own_blocks():
        @pl.when(chip < OWNERS // 2)
        def _():
            for cross, index in ((st_cross, 0), (g_cross, 1)):
                await_arrival(cross, move_swap_sem.at[index])

            @pl.loop(0, CHIPS)
            def _(source):
                for state, gradient, slot in (
                    (st_land.at[source, core], g_land.at[source, core], source * 2 + core),
                    (st_cross.at[source], g_cross.at[source], source * 2 + (1 - core)),
                ):
                    new_fir[slot], new_sec[slot] = moments(
                        state[0].astype(F32), state[1].astype(F32), gradient[...].astype(F32)
                    )

        @pl.when(chip >= OWNERS // 2)
        def _():
            for new in (new_fir, new_sec):
                new[...] = jnp.zeros_like(new)

        pltpu.make_async_copy(new_fir, fir_out, out_sem.at[0]).start()
        pltpu.make_async_copy(new_sec, sec_out, out_sem.at[1]).start()

    reduce_first(0)
    reduce_first(1)
    reduce_first(2)
    pack_state()
    multiply_two()
    multiply_one()
    reduce_second(0)
    reduce_first(3)
    multiply_own()
    reduce_second(1)
    reduce_second(2)
    update(0)
    reduce_second(3)
    update(1)
    forward(0)
    update(2)
    forward(1)
    update(3)
    pl.when(core == 0)(send_gradient)
    forward(2)
    move_across(own_land, own_cross, 2)
    move_across(st_land, st_cross, 0)
    swap(0)
    forward(3)
    pl.when(core == 1)(send_gradient)
    swap(1)
    find_places()
    move_across(g_land, g_cross, 1)
    swap(2)
    swap(3)
    own_blocks()
    settle()

    await_sent(w_out.at[pl.ds(0, 7), 0], rs_send_sem.at[0])
    pltpu.make_async_copy(new_fir, fir_out, out_sem.at[0]).wait()
    pltpu.make_async_copy(new_sec, sec_out, out_sem.at[1]).wait()
    pltpu.make_async_copy(place, where_out, out_sem.at[2]).wait()
    for index, (land, cross) in enumerate(
        ((st_land, st_cross), (g_land, g_cross), (own_land, own_cross))
    ):
        move_sent(land, index)

        @pl.when(chip < OWNERS // 2)
        def _():
            await_sent(cross, move_swap_send_sem.at[index])


def store_kernel(
    w_ref, where_ref, fir_ref, sec_ref, weights, out_mas, out_fir, out_sec, new_mas, places, sem
):
    core = lax.rem(lax.axis_index("shard"), 2)
    where_copy = pltpu.make_async_copy(where_ref, places, sem.at[1])
    where_copy.start()
    copies = [
        pltpu.make_async_copy(
            w_ref.at[s // 2, s % 2], weights.at[:, pl.ds(s * C, C)], sem.at[0]
        )
        for s in range(NS)
    ]
    moved = [
        pltpu.make_async_copy(fir_ref, out_fir, sem.at[2]),
        pltpu.make_async_copy(sec_ref, out_sec, sem.at[3]),
    ]
    for copy in copies + moved:
        copy.start()

    where_copy.wait()

    @pl.loop(0, CHIPS)
    def _(source):
        for index in range(2):
            side = lax.rem(core + index, 2)
            for slot in range(2):
                block = places[index, source, slot]
                held = jnp.maximum(block, 0)
                start = pl.multiple_of(lax.div(held, 2) * 16, 16)
                tile = w_ref[source, side, pl.ds(start, 16)].astype(F32)
                rows = jnp.where(lax.rem(held, 2) == 1, tile[8:16], tile[0:8])
                new_mas[source * 2 + side, pl.ds(slot * 8, 8)] = jnp.where(block >= 0, rows, 0.0)

    moved.append(pltpu.make_async_copy(new_mas, out_mas, sem.at[4]))
    moved[-1].start()
    for copy in moved:
        copy.wait()
    pltpu.make_async_copy(weights, weights, sem.at[0]).wait()


def shards(activations, cotangent, master, adamw_first_moment, second_moment, new_owner):
    tokens = activations.shape[0]
    moved = (NS, SLOT_ROWS, C)
    anywhere = pl.BlockSpec(memory_space=pl.ANY)
    vmem = pl.BlockSpec(memory_space=pltpu.VMEM)
    dma = pltpu.SemaphoreType.DMA
    gathered, where, fir, sec = pl.pallas_call(
        exchange_kernel,
        out_shape=(
            pltpu.VMEM((CHIPS, 2, C, C), BF16),
            pltpu.VMEM((2, CHIPS, 128), jnp.int32),
            pltpu.VMEM(moved, F32),
            pltpu.VMEM(moved, F32),
        ),
        in_specs=[anywhere] * 6,
        out_specs=[anywhere] * 4,
        scratch_shapes=[
            pltpu.VMEM((tokens, C), BF16),
            pltpu.VMEM((NZ, tokens, C), BF16),
            pltpu.VMEM((3, C, C), F32),
            pltpu.VMEM((1, NS), jnp.int32),
            dma((8,)),
            pltpu.VMEM((1, 128), jnp.int32),
            pltpu.VMEM((CHIPS, 1, 128), jnp.int32),
            pltpu.VMEM((CHIPS, 1, 128), jnp.int32),
            pltpu.VMEM((2, CHIPS, 128), jnp.int32),
            pltpu.VMEM((OWNERS * SLOT_ROWS, C), BF16),
            pltpu.VMEM((OWNERS // 2, 2, 2, SLOT_ROWS, C), BF16),
            pltpu.VMEM((CHIPS, 2, 2, SLOT_ROWS, C), BF16),
            pltpu.VMEM((CHIPS, 2, SLOT_ROWS, C), BF16),
            pltpu.VMEM((OWNERS // 2, 2, SLOT_ROWS, C), BF16),
            pltpu.VMEM((CHIPS, 2, SLOT_ROWS, C), BF16),
            pltpu.VMEM((CHIPS, SLOT_ROWS, C), BF16),
            pltpu.VMEM((C, C), BF16),
            pltpu.VMEM((2, C // 2, C), BF16),
            pltpu.VMEM((2, C, C), BF16),
            pltpu.VMEM((2, C, C), BF16),
            pltpu.VMEM((2, C, C), BF16),
            pltpu.VMEM((2, C, C), BF16),
            pltpu.VMEM((2, C, C), BF16),
            pltpu.VMEM((2, C, C), BF16),
            pltpu.VMEM((3, C, C), F32),
            pltpu.VMEM((C, C), BF16),
            pltpu.VMEM((C, C), BF16),
            pltpu.VMEM(moved, F32),
            pltpu.VMEM(moved, F32),
            dma((1,)),
            dma((SUBS,)),
            dma((SUBS,)),
            dma((1,)),
            dma((SUBS, 5)),
            dma((SUBS + 2,)),
            dma((1,)),
            dma((1,)),
            dma((SUBS,)),
            dma((3,)),
            dma((3,)),
            dma((3,)),
            dma((3,)),
            dma((3,)),
        ],
        compiler_params=pltpu.CompilerParams(
            collective_id=0, has_side_effects=True, vmem_limit_bytes=40 * 2**20
        ),
        name="exchange",
    )(
        *[
            pltpu.with_memory_space_constraint(operand, pltpu.HBM)
            for operand in (
                activations, cotangent, master, adamw_first_moment, second_moment,
                new_owner.reshape(1, NS),
            )
        ]
    )
    weights, mas, fir, sec = pl.pallas_call(
        store_kernel,
        out_shape=(
            jax.ShapeDtypeStruct((C, NS * C), BF16),
            jax.ShapeDtypeStruct(moved, F32),
            jax.ShapeDtypeStruct(moved, F32),
            jax.ShapeDtypeStruct(moved, F32),
        ),
        in_specs=[vmem] * 4,
        out_specs=[anywhere] * 4,
        scratch_shapes=[
            pltpu.VMEM(moved, F32),
            pltpu.SMEM((2, CHIPS, 128), jnp.int32),
            dma((5,)),
        ],
        compiler_params=pltpu.CompilerParams(vmem_limit_bytes=8 * 2**20),
        name="store",
    )(
        *[
            pltpu.with_memory_space_constraint(operand, pltpu.VMEM)
            for operand in (gathered, where, fir, sec)
        ]
    )
    out_shape = (1, 1, NS, 2, SLOT_ROWS // 2, C)
    return (weights, mas.reshape(out_shape), fir.reshape(out_shape), sec.reshape(out_shape))


def solution(mesh):
    in_specs = (
        P("dp", "shard"),
        P("dp", None),
        P("dp", "shard"),
        P("dp", "shard"),
        P("dp", "shard"),
        P("dp", "shard", None),
    )
    out_specs = (
        P("dp", None),
        P("dp", "shard", None, None, None, None),
        P("dp", "shard", None, None, None, None),
        P("dp", "shard", None, None, None, None),
    )
    return jax.shard_map(shards, mesh=mesh, in_specs=in_specs, out_specs=out_specs, check_vma=False)
```

```python
import jax
import jax.numpy as jnp
from jax import lax
from jax.experimental import pallas as pl
from jax.experimental.pallas import tpu as pltpu
from jax.sharding import PartitionSpec as P

beta_one = 0.9
beta_two = 0.95
learning_rate = 0.003
decay_rate = 0.1
epsilon_value = 1e-08
adam_step = 100

MESH = pl.DeviceIdType.MESH
BF16 = jnp.bfloat16
F32 = jnp.float32

NZ = 8
ORDER = (4, 3, 5, 2, 6, 1, 7, 0)
NS = 32
CHIPS = 16
OWNERS = 28
SLOT_ROWS = 16
C = 256
ROWS = (64, 64, 64, 64)
SUBS = len(ROWS)
START = tuple(sum(ROWS[:sub]) for sub in range(SUBS))
CROSS = ((1, 0), (-1, 0), (0, 1), (0, -1), (2, 0), (0, 2))
ONWARD = (
    ((0, 1),),
    ((0, -1),),
    ((-1, 0),),
    ((1, 0),),
    ((0, 1), (0, -1)),
    ((1, 0), (-1, 0)),
)


def moments(adamw_first_moment, second_moment, gradient):
    first_new = beta_one * adamw_first_moment + (1.0 - beta_one) * gradient
    second_new = beta_two * second_moment + (1.0 - beta_two) * gradient * gradient
    return first_new, second_new


def adam_update(master, adamw_first_moment, second_moment, gradient):
    corr_one = 1.0 - beta_one**adam_step
    corr_two = 1.0 - beta_two**adam_step
    first_new, second_new = moments(adamw_first_moment, second_moment, gradient)
    direction = first_new / corr_one / (jnp.sqrt(second_new / corr_two) + epsilon_value)
    return master - learning_rate * (direction + decay_rate * master)


def exchange_kernel(
    act_hbm, cot_hbm, mas_hbm, fir_hbm, sec_hbm, own_hbm,
    w_out, where_out, fir_out, sec_out,
    act, cot, state, own, load_sem,
    own_line, own_land, own_cross, place, pick, st_send, st_land, st_cross, g_send, g_land, g_cross,
    far_send, far_recv, mid_send, mid_recv, near_send, near_recv, two_send, two_recv,
    keep, grad, own_w, new_fir, new_sec,
    rs_send_sem, first_sem, last_sem, ag_send_sem, cross_sem, rest_sem, swap_send_sem, swap_sem,
    plane_sem, own_sem, move_send_sem, move_sem, move_swap_send_sem, move_swap_sem, out_sem,
):
    z = lax.axis_index("dp")
    me = lax.axis_index("shard")
    core = lax.rem(me, 2)
    chip = lax.div(me, 2)
    y = lax.rem(chip, 4)
    x = lax.div(chip, 4)

    def at_z(step):
        return lax.rem(z + step + NZ, NZ)

    def plane(dx, dy):
        return lax.rem(x + dx + 4, 4) * 4 + lax.rem(y + dy + 4, 4)

    def on_core(chip_id):
        return (z, chip_id * 2 + core)

    sibling = (z, chip * 2 + (1 - core))

    def remote(src, dst, send_sem, recv_sem, device):
        return pltpu.make_async_remote_copy(
            src_ref=src, dst_ref=dst, send_sem=send_sem, recv_sem=recv_sem,
            device_id=device, device_id_type=MESH,
        )

    def await_sent(ref, sem):
        remote(ref, ref, sem, sem, sibling).wait_send()

    def await_arrival(ref, sem):
        remote(ref, ref, sem, sem, sibling).wait_recv()

    def cot_load(slot):
        start = pl.multiple_of(at_z(ORDER[slot]) * C, C)
        return pltpu.make_async_copy(
            cot_hbm.at[:, pl.ds(start, C)], cot.at[slot], load_sem.at[(slot + 1) // 2]
        )

    def await_cot(slot, count):
        ref = cot.at[pl.ds(slot, count)]
        pltpu.make_async_copy(ref, ref, load_sem.at[(slot + 1) // 2]).wait()

    act_load = pltpu.make_async_copy(act_hbm, act, load_sem.at[5])
    own_load = pltpu.make_async_copy(own_hbm, own, load_sem.at[6])
    mas, fir, sec = state.at[0], state.at[1], state.at[2]
    act_load.start()
    for slot in range(3):
        cot_load(slot).start()

    barrier = pltpu.get_barrier_semaphore()
    row = [on_core(plane(dx, 0)) for dx in (1, 2, 3)]
    column = [on_core(plane(0, dy)) for dy in (1, 2, 3)]
    along_z = [(at_z(step), me) for step in (1, -1, 2, -2)]
    for partner in along_z + [sibling] + row + column:
        pl.semaphore_signal(barrier, inc=1, device_id=partner, device_id_type=MESH)

    def partial(slot):
        return lax.dot_general(
            cot[slot], act[...], (((0,), (0,)), ((), ())), preferred_element_type=F32
        )

    act_load.wait()
    await_cot(0, 1)
    far_send[...] = partial(0).astype(BF16)

    pl.semaphore_wait(barrier, 11)
    for partner in row:
        pl.semaphore_signal(plane_sem, inc=1, device_id=partner, device_id_type=MESH)

    def rows_of(sub):
        return pl.ds(START[sub], ROWS[sub])

    def half_of(sub, way):
        return pl.ds(START[sub] + way * (ROWS[sub] // 2), ROWS[sub] // 2)

    def far_slot(sub):
        return pl.ds(START[sub] // 2, ROWS[sub] // 2)

    def reduce_far(sub):
        for way in (0, 1):
            remote(
                far_send.at[half_of(sub, way)], far_recv.at[way, far_slot(sub)],
                rs_send_sem.at[0], first_sem.at[sub], (at_z(2 - 4 * way), me),
            ).start()

    def reduce_mid(sub):
        for way in (0, 1):
            remote(
                mid_send.at[way, rows_of(sub)], mid_recv.at[way, rows_of(sub)],
                rs_send_sem.at[0], first_sem.at[sub], (at_z(1 - 2 * way), me),
            ).start()

    def multiply_three():
        await_cot(1, 2)
        own_load.start()
        for index, src in enumerate((mas_hbm, fir_hbm, sec_hbm)):
            pltpu.make_async_copy(src, state.at[index], load_sem.at[7]).start()
        for slot in range(3, NZ):
            cot_load(slot).start()
        mid_send[0] = partial(1).astype(BF16)
        mid_send[1] = partial(2).astype(BF16)

    def multiply_two():
        await_cot(3, 2)
        keep[1] = partial(3)
        keep[2] = partial(4)

    def multiply_one():
        await_cot(5, 2)
        near_send[0] = partial(5).astype(BF16)
        near_send[1] = partial(6).astype(BF16)

    def multiply_own():
        await_cot(7, 1)
        keep[0] = partial(7)

    def send_near(sub, way):
        remote(
            near_send.at[way, rows_of(sub)], near_recv.at[way, rows_of(sub)],
            rs_send_sem.at[0], last_sem.at[sub], (at_z(1 - 2 * way), me),
        ).start()

    def reduce_second(sub):
        rows = rows_of(sub)
        await_arrival(w_out.at[pl.ds(0, 3), 0, rows], first_sem.at[sub])
        for way in (0, 1):
            both = half_of(sub, way)
            single = half_of(sub, 1 - way)
            two_send[way, both] = (
                keep[1 + way, both]
                + mid_recv[way, both].astype(F32)
                + far_recv[way, far_slot(sub)].astype(F32)
            ).astype(BF16)
            two_send[way, single] = (
                keep[1 + way, single] + mid_recv[way, single].astype(F32)
            ).astype(BF16)
            remote(
                two_send.at[way, rows], two_recv.at[way, rows], rs_send_sem.at[0],
                last_sem.at[sub], (at_z(2 - 4 * way), me),
            ).start()

    def reduce_near(sub):
        for way in (0, 1):
            send_near(sub, way)

    def packed(values):
        return (
            jnp.dot(pick[...], values, preferred_element_type=F32)
            .astype(BF16)
            .reshape(OWNERS // 2, 2, SLOT_ROWS, C)
        )

    def pack_state():
        own_load.wait()
        pltpu.make_async_copy(state, state, load_sem.at[7]).wait()
        own_line[...] = jnp.full_like(own_line, -1)
        own_line[:, 0:NS] = own[...]
        owner = own[...].astype(F32)
        row_id = lax.broadcasted_iota(jnp.int32, (NS, NS), 0)
        col_id = lax.broadcasted_iota(jnp.int32, (NS, NS), 1)
        wide = jnp.broadcast_to(owner, (NS, NS))
        tall = jnp.sum(jnp.where(row_id == col_id, wide, 0.0), axis=1, keepdims=True)
        rank = jnp.sum(jnp.where((wide == tall) & (row_id < col_id), 1.0, 0.0), axis=0, keepdims=True)
        key = jnp.broadcast_to(owner * 2.0 + rank, (16, NS)).astype(BF16)
        spread = lax.broadcasted_iota(jnp.int32, (NS, C), 0) == lax.div(
            lax.broadcasted_iota(jnp.int32, (NS, C), 1), 8
        )
        slot_of = jnp.dot(key, spread.astype(F32).astype(BF16), preferred_element_type=F32)[0:1]
        within = lax.rem(lax.broadcasted_iota(jnp.int32, (1, C), 1), 8).astype(F32)
        target_row = slot_of * 8.0 + within
        slot_row = lax.broadcasted_iota(jnp.int32, (OWNERS * SLOT_ROWS, C), 0).astype(F32)
        pick[...] = jnp.where(slot_row == target_row, 1.0, 0.0).astype(BF16)

        st_send[:, :, 0] = packed(fir[...].astype(BF16))
        st_send[:, :, 1] = packed(sec[...].astype(BF16))
        pl.semaphore_wait(plane_sem, 3)
        move_out(st_send, st_land, 0)
        move_out(own_line, own_land, 2, lambda to: own_line)

    def move_out(send, land, index, piece=None):
        if piece is None:
            piece = lambda to: send.at[to]

        @pl.loop(1, CHIPS)
        def _(i):
            to = lax.rem(chip + i, CHIPS)

            @pl.when(to < OWNERS // 2)
            def _():
                remote(
                    piece(to), land.at[chip], move_send_sem.at[index], move_sem.at[index],
                    on_core(to),
                ).start()

        @pl.when(chip < OWNERS // 2)
        def _():
            land[chip] = piece(chip)[...]

    def move_across(land, cross, index):
        @pl.when(chip < OWNERS // 2)
        def _():
            await_arrival(land.at[pl.ds(0, CHIPS - 1)], move_sem.at[index])
            remote(
                land if index == 2 else land.at[:, 1 - core], cross,
                move_swap_send_sem.at[index], move_swap_sem.at[index], sibling,
            ).start()

    def move_sent(land, index):
        @pl.when(chip < OWNERS // 2)
        def _():
            await_sent(land.at[pl.ds(0, OWNERS // 2 - 1)], move_send_sem.at[index])

        @pl.when(chip >= OWNERS // 2)
        def _():
            await_sent(land.at[pl.ds(0, OWNERS // 2)], move_send_sem.at[index])

    def gather_send(sub, src, source, to, sem, rows=None):
        dst = w_out.at[source, core, rows_of(sub) if rows is None else rows]
        remote(dst if src is None else src, dst, ag_send_sem.at[0], sem, on_core(to)).start()

    def update(sub):
        rows = rows_of(sub)
        await_arrival(w_out.at[pl.ds(0, 4), 0, rows], last_sem.at[sub])
        total = keep[0, rows]
        for way in (0, 1):
            total = total + near_recv[way, rows].astype(F32) + two_recv[way, rows].astype(F32)
        new_master = adam_update(mas[rows], fir[rows], sec[rows], total)
        own_w[rows] = new_master.astype(BF16)
        for index, (dx, dy) in enumerate(CROSS):
            gather_send(sub, own_w.at[rows], chip, plane(dx, dy), cross_sem.at[sub, min(index, 4)])
        pltpu.make_async_copy(own_w.at[rows], w_out.at[chip, core, rows], own_sem.at[sub]).start()
        if sub == SUBS - 1:
            swap_one(chip, own_w.at[rows])
        grad[rows] = total.astype(BF16)

    def forward(sub):
        for index, (dx, dy) in enumerate(CROSS):
            source = plane(-dx, -dy)
            if index < 4:
                await_arrival(w_out.at[source, core, rows_of(sub)], cross_sem.at[sub, index])
            elif index == 4:
                await_arrival(w_out.at[pl.ds(0, 2), core, rows_of(sub)], cross_sem.at[sub, 4])
            for tx, ty in ONWARD[index]:
                gather_send(sub, None, source, plane(tx, ty), rest_arrival(sub, index // 4))
            if index >= 4:
                gather_send(
                    sub, None, source, plane(dy, dx), rest_arrival(sub, 2), half_of(sub, index - 4)
                )
            if sub == SUBS - 1:
                swap_one(source)

    def rest_arrival(sub, order):
        return rest_sem.at[sub + order if sub == SUBS - 1 else sub]

    def swap_one(source, src=None):
        sub = SUBS - 1
        dst = w_out.at[source, core, rows_of(sub)]
        remote(
            dst if src is None else src, dst, swap_send_sem.at[0], swap_sem.at[0], sibling
        ).start()

    def swap(sub):
        rows = rows_of(sub)
        if sub < SUBS - 1:
            await_arrival(w_out.at[pl.ds(0, 9), 0, rows], rest_sem.at[sub])
            pltpu.make_async_copy(own_w.at[rows], w_out.at[chip, core, rows], own_sem.at[sub]).wait()
            half = w_out.at[:, core, rows]
            remote(half, half, swap_send_sem.at[0], swap_sem.at[0], sibling).start()
            return
        for index, (dx, dy) in enumerate(CROSS):
            if index in (0, 4):
                await_arrival(w_out.at[pl.ds(0, 4), core, rows], rest_arrival(sub, index // 4))
            for tx, ty in ONWARD[index]:
                swap_one(plane(-dx - tx, -dy - ty))
        source = plane(2, 2)
        await_arrival(w_out.at[source, core, rows], rest_arrival(sub, 2))
        swap_one(source)
        pltpu.make_async_copy(own_w.at[rows], w_out.at[chip, core, rows], own_sem.at[sub]).wait()

    def settle():
        await_arrival(w_out.at[:, 1 - core], swap_sem.at[0])
        await_sent(w_out.at[:, core], swap_send_sem.at[0])
        await_sent(w_out.at[pl.ds(0, 15), core], ag_send_sem.at[0])

    def send_gradient():
        g_send[...] = packed(grad[...])
        move_out(g_send, g_land, 1)

    def find_places():
        place[...] = jnp.full_like(place, -1)

        @pl.when(chip < OWNERS // 2)
        def _():
            await_arrival(own_cross, move_swap_sem.at[2])
            lane = lax.broadcasted_iota(jnp.int32, (CHIPS, 128), 1)
            for index, owners in enumerate((own_land, own_cross)):
                mine = owners[...].reshape(CHIPS, 128) == me
                first = jnp.min(jnp.where(mine, lane, 128), axis=1, keepdims=True)
                last = jnp.max(jnp.where(mine, lane, -1), axis=1, keepdims=True)
                place[index] = jnp.where(
                    lane == 0,
                    jnp.where(first < 128, first, -1),
                    jnp.where((lane == 1) & (last > first), last, -1),
                )

        pltpu.make_async_copy(place, where_out, out_sem.at[2]).start()

    def own_blocks():
        @pl.when(chip < OWNERS // 2)
        def _():
            for cross, index in ((st_cross, 0), (g_cross, 1)):
                await_arrival(cross, move_swap_sem.at[index])

            @pl.loop(0, CHIPS)
            def _(source):
                for state, gradient, slot in (
                    (st_land.at[source, core], g_land.at[source, core], source * 2 + core),
                    (st_cross.at[source], g_cross.at[source], source * 2 + (1 - core)),
                ):
                    new_fir[slot], new_sec[slot] = moments(
                        state[0].astype(F32), state[1].astype(F32), gradient[...].astype(F32)
                    )

        @pl.when(chip >= OWNERS // 2)
        def _():
            for new in (new_fir, new_sec):
                new[...] = jnp.zeros_like(new)

        pltpu.make_async_copy(new_fir, fir_out, out_sem.at[0]).start()
        pltpu.make_async_copy(new_sec, sec_out, out_sem.at[1]).start()

    reduce_far(0)
    reduce_far(1)
    reduce_far(2)
    multiply_three()
    reduce_mid(0)
    reduce_mid(1)
    reduce_mid(2)
    multiply_two()
    pack_state()
    multiply_one()
    reduce_second(0)
    reduce_near(0)
    reduce_far(3)
    reduce_mid(3)
    multiply_own()
    reduce_second(1)
    reduce_near(1)
    reduce_second(2)
    reduce_near(2)
    update(0)
    reduce_second(3)
    reduce_near(3)
    update(1)
    forward(0)
    update(2)
    update(3)
    forward(1)
    pl.when(core == 0)(send_gradient)
    forward(2)
    move_across(own_land, own_cross, 2)
    move_across(st_land, st_cross, 0)
    swap(0)
    forward(3)
    pl.when(core == 1)(send_gradient)
    swap(1)
    find_places()
    move_across(g_land, g_cross, 1)
    swap(2)
    swap(3)
    own_blocks()
    settle()

    await_sent(w_out.at[pl.ds(0, 7), 0], rs_send_sem.at[0])
    pltpu.make_async_copy(new_fir, fir_out, out_sem.at[0]).wait()
    pltpu.make_async_copy(new_sec, sec_out, out_sem.at[1]).wait()
    pltpu.make_async_copy(place, where_out, out_sem.at[2]).wait()
    for index, (land, cross) in enumerate(
        ((st_land, st_cross), (g_land, g_cross), (own_land, own_cross))
    ):
        move_sent(land, index)

        @pl.when(chip < OWNERS // 2)
        def _():
            await_sent(cross, move_swap_send_sem.at[index])


def store_kernel(
    w_ref, where_ref, fir_ref, sec_ref, weights, out_mas, out_fir, out_sec, new_mas, places, sem
):
    core = lax.rem(lax.axis_index("shard"), 2)
    where_copy = pltpu.make_async_copy(where_ref, places, sem.at[1])
    where_copy.start()
    copies = [
        pltpu.make_async_copy(
            w_ref.at[s // 2, s % 2], weights.at[:, pl.ds(s * C, C)], sem.at[0]
        )
        for s in range(NS)
    ]
    moved = [
        pltpu.make_async_copy(fir_ref, out_fir, sem.at[2]),
        pltpu.make_async_copy(sec_ref, out_sec, sem.at[3]),
    ]
    for copy in copies + moved:
        copy.start()

    where_copy.wait()

    @pl.loop(0, CHIPS)
    def _(source):
        for index in range(2):
            side = lax.rem(core + index, 2)
            for slot in range(2):
                block = places[index, source, slot]
                held = jnp.maximum(block, 0)
                start = pl.multiple_of(lax.div(held, 2) * 16, 16)
                tile = w_ref[source, side, pl.ds(start, 16)].astype(F32)
                rows = jnp.where(lax.rem(held, 2) == 1, tile[8:16], tile[0:8])
                new_mas[source * 2 + side, pl.ds(slot * 8, 8)] = jnp.where(block >= 0, rows, 0.0)

    moved.append(pltpu.make_async_copy(new_mas, out_mas, sem.at[4]))
    moved[-1].start()
    for copy in moved:
        copy.wait()
    pltpu.make_async_copy(weights, weights, sem.at[0]).wait()


def shards(activations, cotangent, master, adamw_first_moment, second_moment, new_owner):
    tokens = activations.shape[0]
    moved = (NS, SLOT_ROWS, C)
    anywhere = pl.BlockSpec(memory_space=pl.ANY)
    vmem = pl.BlockSpec(memory_space=pltpu.VMEM)
    dma = pltpu.SemaphoreType.DMA
    gathered, where, fir, sec = pl.pallas_call(
        exchange_kernel,
        out_shape=(
            pltpu.VMEM((CHIPS, 2, C, C), BF16),
            pltpu.VMEM((2, CHIPS, 128), jnp.int32),
            pltpu.VMEM(moved, F32),
            pltpu.VMEM(moved, F32),
        ),
        in_specs=[anywhere] * 6,
        out_specs=[anywhere] * 4,
        scratch_shapes=[
            pltpu.VMEM((tokens, C), BF16),
            pltpu.VMEM((NZ, tokens, C), BF16),
            pltpu.VMEM((3, C, C), F32),
            pltpu.VMEM((1, NS), jnp.int32),
            dma((8,)),
            pltpu.VMEM((1, 128), jnp.int32),
            pltpu.VMEM((CHIPS, 1, 128), jnp.int32),
            pltpu.VMEM((CHIPS, 1, 128), jnp.int32),
            pltpu.VMEM((2, CHIPS, 128), jnp.int32),
            pltpu.VMEM((OWNERS * SLOT_ROWS, C), BF16),
            pltpu.VMEM((OWNERS // 2, 2, 2, SLOT_ROWS, C), BF16),
            pltpu.VMEM((CHIPS, 2, 2, SLOT_ROWS, C), BF16),
            pltpu.VMEM((CHIPS, 2, SLOT_ROWS, C), BF16),
            pltpu.VMEM((OWNERS // 2, 2, SLOT_ROWS, C), BF16),
            pltpu.VMEM((CHIPS, 2, SLOT_ROWS, C), BF16),
            pltpu.VMEM((CHIPS, SLOT_ROWS, C), BF16),
            pltpu.VMEM((C, C), BF16),
            pltpu.VMEM((2, C // 2, C), BF16),
            pltpu.VMEM((2, C, C), BF16),
            pltpu.VMEM((2, C, C), BF16),
            pltpu.VMEM((2, C, C), BF16),
            pltpu.VMEM((2, C, C), BF16),
            pltpu.VMEM((2, C, C), BF16),
            pltpu.VMEM((2, C, C), BF16),
            pltpu.VMEM((3, C, C), F32),
            pltpu.VMEM((C, C), BF16),
            pltpu.VMEM((C, C), BF16),
            pltpu.VMEM(moved, F32),
            pltpu.VMEM(moved, F32),
            dma((1,)),
            dma((SUBS,)),
            dma((SUBS,)),
            dma((1,)),
            dma((SUBS, 5)),
            dma((SUBS + 2,)),
            dma((1,)),
            dma((1,)),
            pltpu.SemaphoreType.REGULAR,
            dma((SUBS,)),
            dma((3,)),
            dma((3,)),
            dma((3,)),
            dma((3,)),
            dma((3,)),
        ],
        compiler_params=pltpu.CompilerParams(
            collective_id=0, has_side_effects=True, vmem_limit_bytes=40 * 2**20
        ),
        name="exchange",
    )(
        *[
            pltpu.with_memory_space_constraint(operand, pltpu.HBM)
            for operand in (
                activations, cotangent, master, adamw_first_moment, second_moment,
                new_owner.reshape(1, NS),
            )
        ]
    )
    weights, mas, fir, sec = pl.pallas_call(
        store_kernel,
        out_shape=(
            jax.ShapeDtypeStruct((C, NS * C), BF16),
            jax.ShapeDtypeStruct(moved, F32),
            jax.ShapeDtypeStruct(moved, F32),
            jax.ShapeDtypeStruct(moved, F32),
        ),
        in_specs=[vmem] * 4,
        out_specs=[anywhere] * 4,
        scratch_shapes=[
            pltpu.VMEM(moved, F32),
            pltpu.SMEM((2, CHIPS, 128), jnp.int32),
            dma((5,)),
        ],
        compiler_params=pltpu.CompilerParams(vmem_limit_bytes=8 * 2**20),
        name="store",
    )(
        *[
            pltpu.with_memory_space_constraint(operand, pltpu.VMEM)
            for operand in (gathered, where, fir, sec)
        ]
    )
    out_shape = (1, 1, NS, 2, SLOT_ROWS // 2, C)
    return (weights, mas.reshape(out_shape), fir.reshape(out_shape), sec.reshape(out_shape))


def solution(mesh):
    in_specs = (
        P("dp", "shard"),
        P("dp", None),
        P("dp", "shard"),
        P("dp", "shard"),
        P("dp", "shard"),
        P("dp", "shard", None),
    )
    out_specs = (
        P("dp", None),
        P("dp", "shard", None, None, None, None),
        P("dp", "shard", None, None, None, None),
        P("dp", "shard", None, None, None, None),
    )
    return jax.shard_map(shards, mesh=mesh, in_specs=in_specs, out_specs=out_specs, check_vma=False)
```

```python
import jax
import jax.numpy as jnp
from jax import lax
from jax.experimental import pallas as pl
from jax.experimental.pallas import tpu as pltpu
from jax.sharding import PartitionSpec as P

beta_one = 0.9
beta_two = 0.95
learning_rate = 0.003
decay_rate = 0.1
epsilon_value = 1e-08
adam_step = 100

MESH = pl.DeviceIdType.MESH
BF16 = jnp.bfloat16
F32 = jnp.float32

NZ = 8
ORDER = (4, 3, 5, 2, 6, 1, 7, 0)
NS = 32
CHIPS = 16
OWNERS = 28
SLOT_ROWS = 16
C = 256
ROWS = (64, 64, 64, 64)
SUBS = len(ROWS)
START = tuple(sum(ROWS[:sub]) for sub in range(SUBS))
CROSS = ((1, 0), (-1, 0), (0, 1), (0, -1), (2, 0), (0, 2))
ONWARD = (
    ((0, 1),),
    ((0, -1),),
    ((-1, 0),),
    ((1, 0),),
    ((0, 1), (0, -1)),
    ((1, 0), (-1, 0)),
)


def moments(adamw_first_moment, second_moment, gradient):
    first_new = beta_one * adamw_first_moment + (1.0 - beta_one) * gradient
    second_new = beta_two * second_moment + (1.0 - beta_two) * gradient * gradient
    return first_new, second_new


def adam_update(master, adamw_first_moment, second_moment, gradient):
    corr_one = 1.0 - beta_one**adam_step
    corr_two = 1.0 - beta_two**adam_step
    first_new, second_new = moments(adamw_first_moment, second_moment, gradient)
    direction = first_new / corr_one / (jnp.sqrt(second_new / corr_two) + epsilon_value)
    return master - learning_rate * (direction + decay_rate * master)


def exchange_kernel(
    act_hbm, cot_hbm, mas_hbm, fir_hbm, sec_hbm, own_hbm,
    w_out, where_out, fir_out, sec_out,
    act, cot, state, own, load_sem,
    own_line, own_land, own_cross, place, pick, st_send, st_land, st_cross, g_send, g_land, g_cross,
    far_send, far_recv, mid_send, mid_recv, near_send, near_recv, two_send, two_recv,
    keep, grad, own_w, new_fir, new_sec,
    rs_send_sem, first_sem, last_sem, ag_send_sem, cross_sem, rest_sem, swap_send_sem, swap_sem,
    plane_sem, own_sem, move_send_sem, move_sem, move_swap_send_sem, move_swap_sem, out_sem,
):
    z = lax.axis_index("dp")
    me = lax.axis_index("shard")
    core = lax.rem(me, 2)
    chip = lax.div(me, 2)
    y = lax.rem(chip, 4)
    x = lax.div(chip, 4)

    def at_z(step):
        return lax.rem(z + step + NZ, NZ)

    def plane(dx, dy):
        return lax.rem(x + dx + 4, 4) * 4 + lax.rem(y + dy + 4, 4)

    def on_core(chip_id):
        return (z, chip_id * 2 + core)

    sibling = (z, chip * 2 + (1 - core))

    def remote(src, dst, send_sem, recv_sem, device):
        return pltpu.make_async_remote_copy(
            src_ref=src, dst_ref=dst, send_sem=send_sem, recv_sem=recv_sem,
            device_id=device, device_id_type=MESH,
        )

    def await_sent(ref, sem):
        remote(ref, ref, sem, sem, sibling).wait_send()

    def await_arrival(ref, sem):
        remote(ref, ref, sem, sem, sibling).wait_recv()

    def cot_load(slot):
        start = pl.multiple_of(at_z(ORDER[slot]) * C, C)
        return pltpu.make_async_copy(
            cot_hbm.at[:, pl.ds(start, C)], cot.at[slot], load_sem.at[(slot + 1) // 2]
        )

    def await_cot(slot, count):
        ref = cot.at[pl.ds(slot, count)]
        pltpu.make_async_copy(ref, ref, load_sem.at[(slot + 1) // 2]).wait()

    act_load = pltpu.make_async_copy(act_hbm, act, load_sem.at[5])
    own_load = pltpu.make_async_copy(own_hbm, own, load_sem.at[6])
    mas, fir, sec = state.at[0], state.at[1], state.at[2]
    act_load.start()
    for slot in range(3):
        cot_load(slot).start()

    barrier = pltpu.get_barrier_semaphore()
    row = [on_core(plane(dx, 0)) for dx in (1, 2, 3)]
    column = [on_core(plane(0, dy)) for dy in (1, 2, 3)]
    along_z = [(at_z(step), me) for step in (1, -1, 2, -2)]
    for partner in along_z + [sibling] + row + column:
        pl.semaphore_signal(barrier, inc=1, device_id=partner, device_id_type=MESH)

    def partial(slot):
        return lax.dot_general(
            cot[slot], act[...], (((0,), (0,)), ((), ())), preferred_element_type=F32
        )

    act_load.wait()
    await_cot(0, 1)
    far_send[...] = partial(0).astype(BF16)

    pl.semaphore_wait(barrier, 11)
    for partner in row:
        pl.semaphore_signal(plane_sem, inc=1, device_id=partner, device_id_type=MESH)

    def rows_of(sub):
        return pl.ds(START[sub], ROWS[sub])

    def half_of(sub, way):
        return pl.ds(START[sub] + way * (ROWS[sub] // 2), ROWS[sub] // 2)

    def far_slot(sub):
        return pl.ds(START[sub] // 2, ROWS[sub] // 2)

    def reduce_far(sub):
        for way in (0, 1):
            remote(
                far_send.at[half_of(sub, way)], far_recv.at[way, far_slot(sub)],
                rs_send_sem.at[0], first_sem.at[sub], (at_z(2 - 4 * way), me),
            ).start()

    def reduce_mid(sub):
        for way in (0, 1):
            remote(
                mid_send.at[way, rows_of(sub)], mid_recv.at[way, rows_of(sub)],
                rs_send_sem.at[0], first_sem.at[sub], (at_z(1 - 2 * way), me),
            ).start()

    def multiply_three():
        await_cot(1, 2)
        own_load.start()
        for index, src in enumerate((mas_hbm, fir_hbm, sec_hbm)):
            pltpu.make_async_copy(src, state.at[index], load_sem.at[7]).start()
        for slot in range(3, NZ):
            cot_load(slot).start()
        mid_send[0] = partial(1).astype(BF16)
        mid_send[1] = partial(2).astype(BF16)

    def multiply_two():
        await_cot(3, 2)
        keep[1] = partial(3)
        keep[2] = partial(4)

    def multiply_one():
        await_cot(5, 2)
        near_send[0] = partial(5).astype(BF16)
        near_send[1] = partial(6).astype(BF16)

    def multiply_own():
        await_cot(7, 1)
        keep[0] = partial(7)

    def send_near(sub, way):
        remote(
            near_send.at[way, rows_of(sub)], near_recv.at[way, rows_of(sub)],
            rs_send_sem.at[0], last_sem.at[sub], (at_z(1 - 2 * way), me),
        ).start()

    def reduce_second(sub):
        rows = rows_of(sub)
        await_arrival(w_out.at[pl.ds(0, 3), 0, rows], first_sem.at[sub])
        for way in (0, 1):
            both = half_of(sub, way)
            single = half_of(sub, 1 - way)
            two_send[way, both] = (
                keep[1 + way, both]
                + mid_recv[way, both].astype(F32)
                + far_recv[way, far_slot(sub)].astype(F32)
            ).astype(BF16)
            two_send[way, single] = (
                keep[1 + way, single] + mid_recv[way, single].astype(F32)
            ).astype(BF16)
            remote(
                two_send.at[way, rows], two_recv.at[way, rows], rs_send_sem.at[0],
                last_sem.at[sub], (at_z(2 - 4 * way), me),
            ).start()

    def reduce_near(sub):
        for way in (0, 1):
            send_near(sub, way)

    def packed(values):
        return (
            jnp.dot(pick[...], values, preferred_element_type=F32)
            .astype(BF16)
            .reshape(OWNERS // 2, 2, SLOT_ROWS, C)
        )

    def pack_state():
        own_load.wait()
        pltpu.make_async_copy(state, state, load_sem.at[7]).wait()
        own_line[...] = jnp.full_like(own_line, -1)
        own_line[:, 0:NS] = own[...]
        owner = own[...].astype(F32)
        row_id = lax.broadcasted_iota(jnp.int32, (NS, NS), 0)
        col_id = lax.broadcasted_iota(jnp.int32, (NS, NS), 1)
        wide = jnp.broadcast_to(owner, (NS, NS))
        tall = jnp.sum(jnp.where(row_id == col_id, wide, 0.0), axis=1, keepdims=True)
        rank = jnp.sum(jnp.where((wide == tall) & (row_id < col_id), 1.0, 0.0), axis=0, keepdims=True)
        key = jnp.broadcast_to(owner * 2.0 + rank, (16, NS)).astype(BF16)
        spread = lax.broadcasted_iota(jnp.int32, (NS, C), 0) == lax.div(
            lax.broadcasted_iota(jnp.int32, (NS, C), 1), 8
        )
        slot_of = jnp.dot(key, spread.astype(F32).astype(BF16), preferred_element_type=F32)[0:1]
        within = lax.rem(lax.broadcasted_iota(jnp.int32, (1, C), 1), 8).astype(F32)
        target_row = slot_of * 8.0 + within
        slot_row = lax.broadcasted_iota(jnp.int32, (OWNERS * SLOT_ROWS, C), 0).astype(F32)
        pick[...] = jnp.where(slot_row == target_row, 1.0, 0.0).astype(BF16)

        st_send[:, :, 0] = packed(fir[...].astype(BF16))
        st_send[:, :, 1] = packed(sec[...].astype(BF16))
        pl.semaphore_wait(plane_sem, 3)
        move_out(st_send, st_land, 0)
        move_out(own_line, own_land, 2, lambda to: own_line)

    def move_out(send, land, index, piece=None):
        if piece is None:
            piece = lambda to: send.at[to]

        @pl.loop(1, CHIPS)
        def _(i):
            to = lax.rem(chip + i, CHIPS)

            @pl.when(to < OWNERS // 2)
            def _():
                remote(
                    piece(to), land.at[chip], move_send_sem.at[index], move_sem.at[index],
                    on_core(to),
                ).start()

        @pl.when(chip < OWNERS // 2)
        def _():
            land[chip] = piece(chip)[...]

    def move_across(land, cross, index):
        @pl.when(chip < OWNERS // 2)
        def _():
            await_arrival(land.at[pl.ds(0, CHIPS - 1)], move_sem.at[index])
            remote(
                land if index == 2 else land.at[:, 1 - core], cross,
                move_swap_send_sem.at[index], move_swap_sem.at[index], sibling,
            ).start()

    def move_sent(land, index):
        @pl.when(chip < OWNERS // 2)
        def _():
            await_sent(land.at[pl.ds(0, OWNERS // 2 - 1)], move_send_sem.at[index])

        @pl.when(chip >= OWNERS // 2)
        def _():
            await_sent(land.at[pl.ds(0, OWNERS // 2)], move_send_sem.at[index])

    def gather_send(sub, src, source, to, sem, rows=None):
        dst = w_out.at[source, core, rows_of(sub) if rows is None else rows]
        remote(dst if src is None else src, dst, ag_send_sem.at[0], sem, on_core(to)).start()

    def update(sub):
        rows = rows_of(sub)
        await_arrival(w_out.at[pl.ds(0, 4), 0, rows], last_sem.at[sub])
        total = keep[0, rows]
        for way in (0, 1):
            total = total + near_recv[way, rows].astype(F32) + two_recv[way, rows].astype(F32)
        new_master = adam_update(mas[rows], fir[rows], sec[rows], total)
        own_w[rows] = new_master.astype(BF16)
        for index, (dx, dy) in enumerate(CROSS):
            gather_send(sub, own_w.at[rows], chip, plane(dx, dy), cross_sem.at[sub, index // 4])
        pltpu.make_async_copy(own_w.at[rows], w_out.at[chip, core, rows], own_sem.at[sub]).start()
        if sub == SUBS - 1:
            swap_one(chip, own_w.at[rows])
        grad[rows] = total.astype(BF16)

    def forward(sub):
        for index, (dx, dy) in enumerate(CROSS):
            source = plane(-dx, -dy)
            if index in (0, 4):
                count = 4 - index // 2
                await_arrival(
                    w_out.at[pl.ds(0, count), core, rows_of(sub)], cross_sem.at[sub, index // 4]
                )
            for tx, ty in ONWARD[index]:
                gather_send(sub, None, source, plane(tx, ty), rest_arrival(sub, index // 4))
            if index >= 4:
                gather_send(
                    sub, None, source, plane(dy, dx), rest_arrival(sub, 2), half_of(sub, index - 4)
                )
            if sub == SUBS - 1:
                swap_one(source)

    def rest_arrival(sub, order):
        return rest_sem.at[sub + order if sub == SUBS - 1 else sub]

    def swap_one(source, src=None):
        sub = SUBS - 1
        dst = w_out.at[source, core, rows_of(sub)]
        remote(
            dst if src is None else src, dst, swap_send_sem.at[0], swap_sem.at[0], sibling
        ).start()

    def swap(sub):
        rows = rows_of(sub)
        if sub < SUBS - 1:
            await_arrival(w_out.at[pl.ds(0, 9), 0, rows], rest_sem.at[sub])
            pltpu.make_async_copy(own_w.at[rows], w_out.at[chip, core, rows], own_sem.at[sub]).wait()
            half = w_out.at[:, core, rows]
            remote(half, half, swap_send_sem.at[0], swap_sem.at[0], sibling).start()
            return
        for index, (dx, dy) in enumerate(CROSS):
            if index in (0, 4):
                await_arrival(w_out.at[pl.ds(0, 4), core, rows], rest_arrival(sub, index // 4))
            for tx, ty in ONWARD[index]:
                swap_one(plane(-dx - tx, -dy - ty))
        source = plane(2, 2)
        await_arrival(w_out.at[source, core, rows], rest_arrival(sub, 2))
        swap_one(source)
        pltpu.make_async_copy(own_w.at[rows], w_out.at[chip, core, rows], own_sem.at[sub]).wait()

    def settle():
        await_arrival(w_out.at[:, 1 - core], swap_sem.at[0])
        await_sent(w_out.at[:, core], swap_send_sem.at[0])
        await_sent(w_out.at[pl.ds(0, 15), core], ag_send_sem.at[0])

    def send_gradient():
        g_send[...] = packed(grad[...])
        move_out(g_send, g_land, 1)

    def find_places():
        place[...] = jnp.full_like(place, -1)

        @pl.when(chip < OWNERS // 2)
        def _():
            await_arrival(own_cross, move_swap_sem.at[2])
            lane = lax.broadcasted_iota(jnp.int32, (CHIPS, 128), 1)
            for index, owners in enumerate((own_land, own_cross)):
                mine = owners[...].reshape(CHIPS, 128) == me
                first = jnp.min(jnp.where(mine, lane, 128), axis=1, keepdims=True)
                last = jnp.max(jnp.where(mine, lane, -1), axis=1, keepdims=True)
                place[index] = jnp.where(
                    lane == 0,
                    jnp.where(first < 128, first, -1),
                    jnp.where((lane == 1) & (last > first), last, -1),
                )

        pltpu.make_async_copy(place, where_out, out_sem.at[2]).start()

    def own_blocks():
        @pl.when(chip < OWNERS // 2)
        def _():
            for cross, index in ((st_cross, 0), (g_cross, 1)):
                await_arrival(cross, move_swap_sem.at[index])

            @pl.loop(0, CHIPS)
            def _(source):
                for state, gradient, slot in (
                    (st_land.at[source, core], g_land.at[source, core], source * 2 + core),
                    (st_cross.at[source], g_cross.at[source], source * 2 + (1 - core)),
                ):
                    new_fir[slot], new_sec[slot] = moments(
                        state[0].astype(F32), state[1].astype(F32), gradient[...].astype(F32)
                    )

        @pl.when(chip >= OWNERS // 2)
        def _():
            for new in (new_fir, new_sec):
                new[...] = jnp.zeros_like(new)

        pltpu.make_async_copy(new_fir, fir_out, out_sem.at[0]).start()
        pltpu.make_async_copy(new_sec, sec_out, out_sem.at[1]).start()

    reduce_far(0)
    reduce_far(1)
    reduce_far(2)
    multiply_three()
    reduce_mid(0)
    reduce_mid(1)
    reduce_mid(2)
    multiply_two()
    pack_state()
    multiply_one()
    reduce_second(0)
    reduce_near(0)
    reduce_far(3)
    reduce_mid(3)
    multiply_own()
    reduce_second(1)
    reduce_near(1)
    reduce_second(2)
    reduce_near(2)
    update(0)
    reduce_second(3)
    reduce_near(3)
    update(1)
    forward(0)
    update(2)
    update(3)
    forward(1)
    pl.when(core == 0)(send_gradient)
    forward(2)
    move_across(own_land, own_cross, 2)
    move_across(st_land, st_cross, 0)
    swap(0)
    forward(3)
    pl.when(core == 1)(send_gradient)
    swap(1)
    find_places()
    move_across(g_land, g_cross, 1)
    swap(2)
    swap(3)
    own_blocks()
    settle()

    await_sent(w_out.at[pl.ds(0, 7), 0], rs_send_sem.at[0])
    pltpu.make_async_copy(new_fir, fir_out, out_sem.at[0]).wait()
    pltpu.make_async_copy(new_sec, sec_out, out_sem.at[1]).wait()
    pltpu.make_async_copy(place, where_out, out_sem.at[2]).wait()
    for index, (land, cross) in enumerate(
        ((st_land, st_cross), (g_land, g_cross), (own_land, own_cross))
    ):
        move_sent(land, index)

        @pl.when(chip < OWNERS // 2)
        def _():
            await_sent(cross, move_swap_send_sem.at[index])


def store_kernel(
    w_ref, where_ref, fir_ref, sec_ref, weights, out_mas, out_fir, out_sec, new_mas, places, sem
):
    core = lax.rem(lax.axis_index("shard"), 2)
    where_copy = pltpu.make_async_copy(where_ref, places, sem.at[1])
    where_copy.start()
    copies = [
        pltpu.make_async_copy(
            w_ref.at[s // 2, s % 2], weights.at[:, pl.ds(s * C, C)], sem.at[0]
        )
        for s in range(NS)
    ]
    moved = [
        pltpu.make_async_copy(fir_ref, out_fir, sem.at[2]),
        pltpu.make_async_copy(sec_ref, out_sec, sem.at[3]),
    ]
    for copy in copies + moved:
        copy.start()

    where_copy.wait()

    @pl.loop(0, CHIPS)
    def _(source):
        for index in range(2):
            side = lax.rem(core + index, 2)
            for slot in range(2):
                block = places[index, source, slot]
                held = jnp.maximum(block, 0)
                start = pl.multiple_of(lax.div(held, 2) * 16, 16)
                tile = w_ref[source, side, pl.ds(start, 16)].astype(F32)
                rows = jnp.where(lax.rem(held, 2) == 1, tile[8:16], tile[0:8])
                new_mas[source * 2 + side, pl.ds(slot * 8, 8)] = jnp.where(block >= 0, rows, 0.0)

    moved.append(pltpu.make_async_copy(new_mas, out_mas, sem.at[4]))
    moved[-1].start()
    for copy in moved:
        copy.wait()
    pltpu.make_async_copy(weights, weights, sem.at[0]).wait()


def shards(activations, cotangent, master, adamw_first_moment, second_moment, new_owner):
    tokens = activations.shape[0]
    moved = (NS, SLOT_ROWS, C)
    anywhere = pl.BlockSpec(memory_space=pl.ANY)
    vmem = pl.BlockSpec(memory_space=pltpu.VMEM)
    dma = pltpu.SemaphoreType.DMA
    gathered, where, fir, sec = pl.pallas_call(
        exchange_kernel,
        out_shape=(
            pltpu.VMEM((CHIPS, 2, C, C), BF16),
            pltpu.VMEM((2, CHIPS, 128), jnp.int32),
            pltpu.VMEM(moved, F32),
            pltpu.VMEM(moved, F32),
        ),
        in_specs=[anywhere] * 6,
        out_specs=[anywhere] * 4,
        scratch_shapes=[
            pltpu.VMEM((tokens, C), BF16),
            pltpu.VMEM((NZ, tokens, C), BF16),
            pltpu.VMEM((3, C, C), F32),
            pltpu.VMEM((1, NS), jnp.int32),
            dma((8,)),
            pltpu.VMEM((1, 128), jnp.int32),
            pltpu.VMEM((CHIPS, 1, 128), jnp.int32),
            pltpu.VMEM((CHIPS, 1, 128), jnp.int32),
            pltpu.VMEM((2, CHIPS, 128), jnp.int32),
            pltpu.VMEM((OWNERS * SLOT_ROWS, C), BF16),
            pltpu.VMEM((OWNERS // 2, 2, 2, SLOT_ROWS, C), BF16),
            pltpu.VMEM((CHIPS, 2, 2, SLOT_ROWS, C), BF16),
            pltpu.VMEM((CHIPS, 2, SLOT_ROWS, C), BF16),
            pltpu.VMEM((OWNERS // 2, 2, SLOT_ROWS, C), BF16),
            pltpu.VMEM((CHIPS, 2, SLOT_ROWS, C), BF16),
            pltpu.VMEM((CHIPS, SLOT_ROWS, C), BF16),
            pltpu.VMEM((C, C), BF16),
            pltpu.VMEM((2, C // 2, C), BF16),
            pltpu.VMEM((2, C, C), BF16),
            pltpu.VMEM((2, C, C), BF16),
            pltpu.VMEM((2, C, C), BF16),
            pltpu.VMEM((2, C, C), BF16),
            pltpu.VMEM((2, C, C), BF16),
            pltpu.VMEM((2, C, C), BF16),
            pltpu.VMEM((3, C, C), F32),
            pltpu.VMEM((C, C), BF16),
            pltpu.VMEM((C, C), BF16),
            pltpu.VMEM(moved, F32),
            pltpu.VMEM(moved, F32),
            dma((1,)),
            dma((SUBS,)),
            dma((SUBS,)),
            dma((1,)),
            dma((SUBS, 2)),
            dma((SUBS + 2,)),
            dma((1,)),
            dma((1,)),
            pltpu.SemaphoreType.REGULAR,
            dma((SUBS,)),
            dma((3,)),
            dma((3,)),
            dma((3,)),
            dma((3,)),
            dma((3,)),
        ],
        compiler_params=pltpu.CompilerParams(
            collective_id=0, has_side_effects=True, vmem_limit_bytes=40 * 2**20
        ),
        name="exchange",
    )(
        *[
            pltpu.with_memory_space_constraint(operand, pltpu.HBM)
            for operand in (
                activations, cotangent, master, adamw_first_moment, second_moment,
                new_owner.reshape(1, NS),
            )
        ]
    )
    weights, mas, fir, sec = pl.pallas_call(
        store_kernel,
        out_shape=(
            jax.ShapeDtypeStruct((C, NS * C), BF16),
            jax.ShapeDtypeStruct(moved, F32),
            jax.ShapeDtypeStruct(moved, F32),
            jax.ShapeDtypeStruct(moved, F32),
        ),
        in_specs=[vmem] * 4,
        out_specs=[anywhere] * 4,
        scratch_shapes=[
            pltpu.VMEM(moved, F32),
            pltpu.SMEM((2, CHIPS, 128), jnp.int32),
            dma((5,)),
        ],
        compiler_params=pltpu.CompilerParams(vmem_limit_bytes=8 * 2**20),
        name="store",
    )(
        *[
            pltpu.with_memory_space_constraint(operand, pltpu.VMEM)
            for operand in (gathered, where, fir, sec)
        ]
    )
    out_shape = (1, 1, NS, 2, SLOT_ROWS // 2, C)
    return (weights, mas.reshape(out_shape), fir.reshape(out_shape), sec.reshape(out_shape))


def solution(mesh):
    in_specs = (
        P("dp", "shard"),
        P("dp", None),
        P("dp", "shard"),
        P("dp", "shard"),
        P("dp", "shard"),
        P("dp", "shard", None),
    )
    out_specs = (
        P("dp", None),
        P("dp", "shard", None, None, None, None),
        P("dp", "shard", None, None, None, None),
        P("dp", "shard", None, None, None, None),
    )
    return jax.shard_map(shards, mesh=mesh, in_specs=in_specs, out_specs=out_specs, check_vma=False)
```
